32 devices in a mesh: dom: 4 (over y, core), spec: 8 (over z, x).
Axes of the slice: x: 2, y: 2, z: 4, core: 2. Of those that a mesh axis runs over, the one named last changes fastest.
Arguments:
- spectrum: float32 [256, 131072], P('spec', 'dom'), may hold values from -6 to 6
- conductance: float32 [256, 131072], P(None, ('dom', 'spec')), may hold values from 0.05 to 2
- capacitance: float32 [256, 131072], P(None, ('dom', 'spec')), may hold values from 0.05 to 2
- block_cond: float32 [1024, 128, 128], P(('dom', 'spec')), may hold values from -0.5 to 0.5
- block_cap: float32 [1024, 128, 128], P(('dom', 'spec')), may hold values from -0.5 to 0.5
- boundary_nodes: int32 [4, 128], P('dom'), may hold values from 0 to 32767, as said below
- couple_src: int32 [4, 3], P('dom'), may hold values from 0 to 3, as said below
- couple_count: int32 [4], P('dom'), may hold values from 1 to 3, as said below
- couple_cond: float32 [4, 3, 128, 128], P('dom'), may hold values from -0.5 to 0.5
- couple_cap: float32 [4, 3, 128, 128], P('dom'), may hold values from -0.5 to 0.5
Outputs:
- jacobian_product: float32 [256, 131072], P('spec', 'dom')
The draws below stay inside these ranges and needn't reach their ends.
Inputs may be any that keep to these rules, and one draw needn't show every extreme that they name: `boundary_nodes`: row d lists 128 distinct nodes of partition d; entries 16 * s to 16 * (s + 1) - 1 lie among nodes 4096 * s to 4096 * (s + 1) - 1 and increase. `couple_src`: row d holds every partition other than d once. Partition d uses the first couple_count[d] entries of its rows of couple_src, couple_cond and couple_cap; some partition uses all 3.
All inputs are finite; a program needn't handle non-finite values.
Results may differ from the reference program's by a relative error of at most 0.0001.
Values sent between devices are 32-bit elements; how exact they have to be, the bound alone decides.
A program may use at most 192 MiB of HBM per device.

```python
import math
import jax
import jax.numpy as jnp
from jax import lax

S = 256
BS = 128
ND = 4096
BPD = 16
NP = 32768
NODES = 131072
NBLK = 1024
NBND = 128
MAXC = 3
N_DOM = 4


def draw_boundary_nodes(key, part):
    slices = NBND // BPD
    key_list = jax.random.split(key, N_DOM * slices)

    def pick_nodes(one_key):
        return jnp.sort(jax.random.permutation(one_key, ND)[:BPD])
    picked = jax.vmap(pick_nodes)(key_list).astype(jnp.int32)
    offsets = jnp.arange(N_DOM * slices, dtype=jnp.int32) % slices * ND
    return (picked + offsets[:, None]).reshape(N_DOM, NBND).astype(jnp.int32)


def draw_couple_src(key, part):
    key_list = jax.random.split(key, N_DOM)

    def one_row(one_key, owner_id):
        shuffled = jax.random.permutation(one_key, MAXC).astype(jnp.int32)
        return shuffled + (shuffled >= owner_id).astype(jnp.int32)
    return jax.vmap(one_row)(key_list, jnp.arange(N_DOM, dtype=jnp.int32)).astype(jnp.int32)


def draw_couple_count(key, part):
    counts = jax.random.randint(key, (N_DOM,), 1, MAXC + 1)
    fullest = jax.random.randint(jax.random.fold_in(key, 7), (), 0, N_DOM)
    return counts.at[fullest].set(MAXC).astype(jnp.int32)


def block_scale(stream_key, dims, cuts, smallest, top_value):
    def one(position, blocks):
        steps = jax.random.uniform(jax.random.fold_in(jax.random.fold_in(stream_key, 6), position), (blocks,), jnp.float32, smallest / len(cuts), top_value / len(cuts))
        return jnp.repeat(jnp.exp(steps), dims[position] // blocks).reshape((-1,) + (1,) * (len(dims) - position - 1))

    gain = one(*cuts[0])
    for cut in cuts[1:]:
        gain = gain * one(*cut)
    return gain


def bell_draw(own_key, shape, scale, reach, cuts=(), held_as=jnp.bfloat16):
    values = jax.random.normal(own_key, shape, jnp.float32) * scale
    if len(cuts) > 0:
        values = block_scale(own_key, shape, cuts, -0.22, 0.18) * values
    return jnp.clip(values, min=-reach, max=reach).astype(held_as)


def setup_inputs(seed: int = 0) -> dict:
    seeds = jax.random.split(jax.random.key(seed), 11)
    spectrum = bell_draw(seeds[0], (S, NODES), 1.0, 6.0, ((0, 8), (1, 4)), jnp.float32)
    conductance = jnp.clip(jnp.exp(math.log(2.0) - 3.6888794 * jax.random.uniform(seeds[1], (S, NODES), jnp.float32) ** block_scale(seeds[1], (S, NODES), ((1, 32),), -0.2, 0.2)), 0.05, 2.0)
    capacitance = jnp.clip(jnp.exp(math.log(2.0) - 3.6888794 * jax.random.uniform(seeds[2], (S, NODES), jnp.float32) ** block_scale(seeds[2], (S, NODES), ((1, 32),), -0.2, 0.2)), 0.05, 2.0)
    block_cond = bell_draw(seeds[3], (NBLK, BS, BS), BS ** -0.5, 0.5, ((0, 32),), jnp.float32)
    block_cap = bell_draw(seeds[4], (NBLK, BS, BS), BS ** -0.5, 0.5, ((0, 32),), jnp.float32)
    boundary_nodes = draw_boundary_nodes(jax.random.fold_in(seeds[10], 71), 0)
    couple_src = draw_couple_src(jax.random.fold_in(seeds[10], 71), 0)
    couple_count = draw_couple_count(jax.random.fold_in(seeds[10], 71), 0)
    couple_cond = bell_draw(seeds[8], (N_DOM, MAXC, NBND, NBND), NBND ** -0.5, 0.5, ((0, 4),), jnp.float32)
    couple_cap = bell_draw(seeds[9], (N_DOM, MAXC, NBND, NBND), NBND ** -0.5, 0.5, ((0, 4),), jnp.float32)
    return dict(spectrum=spectrum, conductance=conductance, capacitance=capacitance, block_cond=block_cond, block_cap=block_cap, boundary_nodes=boundary_nodes, couple_src=couple_src, couple_count=couple_count, couple_cond=couple_cond, couple_cap=couple_cap)


HIGHEST = lax.Precision.HIGHEST


def fourier_tables(length):
    time_ids = jnp.arange(length, dtype=jnp.int32)
    column_ids = jnp.arange(length, dtype=jnp.int32)
    harmonic = jnp.where(column_ids == 1, length // 2, column_ids // 2)
    phase_ids = (time_ids[:, None] * harmonic[None, :]) % length
    angles = phase_ids.astype(jnp.float32) * jnp.float32(2.0 * math.pi / length)
    is_sine = (column_ids % 2 == 1) & (column_ids >= 2)
    basis_table = jnp.where(is_sine[None, :], jnp.sin(angles), jnp.cos(angles))
    row_scale = jnp.where(column_ids < 2, 1.0 / length, 2.0 / length).astype(jnp.float32)
    forward = basis_table.T * row_scale[:, None]
    return basis_table, forward


def derivative(spectra_in, first_row, length):
    row_count = spectra_in.shape[0]
    paired = spectra_in.reshape((row_count // 2, 2) + spectra_in.shape[1:])
    pair_ids = first_row // 2 + jnp.arange(row_count // 2, dtype=jnp.int32)
    frequency = jnp.where(pair_ids >= 1, pair_ids.astype(jnp.float32) * (2.0 / length), 0.0).astype(jnp.float32)
    frequency = frequency.reshape((row_count // 2,) + (1,) * (spectra_in.ndim - 1))
    even_part = paired[:, 0]
    odd_part = paired[:, 1]
    return jnp.stack([frequency * odd_part, -frequency * even_part], axis=1).reshape(spectra_in.shape)


def network(spectra_in, slopes, block_cond, block_cap):
    length, node_count = spectra_in.shape
    block_size = block_cond.shape[1]
    shaped = spectra_in.reshape(length, node_count // block_size, block_size)
    shaped_slope = slopes.reshape(length, node_count // block_size, block_size)
    result = jnp.einsum('mbj,bij->mbi', shaped, block_cond, precision=HIGHEST)
    result = result + jnp.einsum('mbj,bij->mbi', shaped_slope, block_cap, precision=HIGHEST)
    return result.reshape(length, node_count)


def couple(gathered, first_row, length, sources, used, rows_cond, rows_cap):
    slopes = derivative(gathered, first_row, length)
    owners = jnp.arange(gathered.shape[1], dtype=jnp.int32)
    slot_ids = jnp.arange(sources.shape[0], dtype=jnp.int32)
    chosen = ((sources[:, None] == owners[None, :]) & (slot_ids < used)[:, None]).astype(jnp.float32)
    source_values = jnp.einsum('cp,mpk->cmk', chosen, gathered, precision=HIGHEST)
    source_slopes = jnp.einsum('cp,mpk->cmk', chosen, slopes, precision=HIGHEST)
    current = jnp.einsum('cmk,cjk->mj', source_values, rows_cond, precision=HIGHEST)
    return current + jnp.einsum('cmk,cjk->mj', source_slopes, rows_cap, precision=HIGHEST)


def reference(spectrum, conductance, capacitance, block_cond, block_cap, boundary_nodes, couple_src, couple_count, couple_cond, couple_cap):
    basis_table, forward = fourier_tables(S)
    waveforms = jnp.dot(basis_table, spectrum, precision=HIGHEST)
    device_current = jnp.dot(forward, conductance * waveforms, precision=HIGHEST)
    device_current = device_current + derivative(jnp.dot(forward, capacitance * waveforms, precision=HIGHEST), 0, S)
    slope_spec = derivative(spectrum, 0, S)
    summed = device_current + network(spectrum, slope_spec, block_cond, block_cap)
    partitions_view = spectrum.reshape(S, N_DOM, NP)
    bound_spec = partitions_view[:, jnp.arange(N_DOM, dtype=jnp.int32)[:, None], boundary_nodes]
    summed = summed.reshape(S, N_DOM, NP)
    for partition in range(N_DOM):
        current = couple(bound_spec, 0, S, couple_src[partition], couple_count[partition], couple_cond[partition], couple_cap[partition])
        summed = summed.at[:, partition, boundary_nodes[partition]].add(current)
    return summed.reshape(S, NODES)
```

```python
import functools
import math

import jax
import jax.numpy as jnp
import ml_dtypes
import numpy as np
from jax import lax
from jax.experimental import pallas as pl
from jax.experimental.pallas import tpu as pltpu
from jax.sharding import PartitionSpec as P

MESH = pl.DeviceIdType.MESH
CHUNK = 512
GATHER = 2048
f32 = jnp.float32
bf16 = jnp.bfloat16


def split_table(table):
    high = table.astype(ml_dtypes.bfloat16)
    low = (table - high.astype(np.float64)).astype(ml_dtypes.bfloat16)
    return high, low


def fourier_tables(length):
    ids = np.arange(length)
    harmonic = np.where(ids == 1, length // 2, ids // 2)
    phase = (ids[:, None] * harmonic[None, :]) % length
    angles = phase * (2.0 * math.pi / length)
    is_sine = (ids % 2 == 1) & (ids >= 2)
    basis = np.where(is_sine[None, :], np.sin(angles), np.cos(angles))
    forward = basis.T * np.where(ids < 2, 1.0 / length, 2.0 / length)[:, None]
    frequency = np.where(ids >= 2, (ids // 2) * (2.0 / length), 0.0)[:, None]
    swapped = forward.reshape(length // 2, 2, length)[:, ::-1].reshape(length, length)
    slope = np.where((ids % 2 == 0)[:, None], frequency, -frequency) * swapped
    return split_table(basis) + split_table(np.concatenate([forward, slope], axis=1))


def split(values):
    high = values.astype(bf16)
    return high, (values - high.astype(f32)).astype(bf16)


def dot3(left, right, dims=(((1,), (0,)), ((), ()))):
    dot = functools.partial(lax.dot_general, dimension_numbers=dims, preferred_element_type=f32)
    return dot(left[0], right[0]) + (dot(left[0], right[1]) + dot(left[1], right[0]))


BOTH_LANES = (((1,), (1,)), ((), ()))


def derivative(values, first_row, length):
    rows = values.shape[0]
    ids = first_row + lax.broadcasted_iota(jnp.int32, (rows, 1), 0)
    frequency = (ids // 2).astype(f32) * (2.0 / length)
    even = ids % 2 == 0
    from_next = jnp.where(even, frequency, 0.0)
    from_last = jnp.where(even, 0.0, -frequency)
    return from_next * pltpu.roll(values, rows - 1, 0) + from_last * pltpu.roll(values, 1, 0)


def kernel(
    n_dom,
    n_spec,
    spectrum,
    cond,
    cap,
    block_cond,
    block_cap,
    bound,
    sources,
    used,
    couple_cond,
    couple_cap,
    basis_h,
    basis_l,
    fwd_h,
    fwd_l,
    out,
    x_all,
    y_all,
    o_all,
    spec_v,
    cond_v,
    cap_v,
    bcond_v,
    bcap_v,
    ccond_v,
    ccap_v,
    basis_hv,
    basis_lv,
    fwd_hv,
    fwd_lv,
    gathered,
    bound_col,
    current,
    load_sem,
    own_sem,
    keep_sem,
    out_sem,
    go_send,
    go_recv,
    back_send,
    back_recv,
    dom_send,
    dom_recv,
):
    rows = spectrum.shape[0]
    length, nodes = cond.shape
    n_bound = bound.shape[1]
    n_chunks = nodes // CHUNK
    dom = lax.axis_index("dom")
    me = lax.axis_index("spec")
    my_row = pl.multiple_of(me * rows, rows)

    def spec_peer(k):
        return lax.rem(me + k, n_spec)

    barrier = pltpu.get_barrier_semaphore()
    for k in range(1, n_spec):
        pl.semaphore_signal(barrier, inc=1, device_id=(dom, spec_peer(k)), device_id_type=MESH)
    for k in range(1, n_dom):
        pl.semaphore_signal(
            barrier, inc=1, device_id=(lax.rem(dom + k, n_dom), me), device_id_type=MESH
        )
    pl.semaphore_wait(barrier, n_spec - 1 + n_dom - 1)

    def lanes(first, size):
        return pl.ds(pl.multiple_of(first, size), size)

    def send_go(c, carry):
        for k in range(1, n_spec):
            peer = spec_peer(k)
            pltpu.make_async_remote_copy(
                src_ref=spectrum.at[:, lanes(peer * nodes + c * CHUNK, CHUNK)],
                dst_ref=x_all.at[pl.ds(my_row, rows), lanes(c * CHUNK, CHUNK)],
                send_sem=go_send,
                recv_sem=go_recv.at[c],
                device_id=(dom, peer),
                device_id_type=MESH,
            ).start()
        return carry

    lax.fori_loop(0, n_chunks, send_go, 0)

    loads = [
        pltpu.make_async_copy(source, target, load_sem.at[i])
        for i, (source, target) in enumerate(
            [
                (spectrum, spec_v),
                (couple_cond, ccond_v),
                (couple_cap, ccap_v),
                (basis_h, basis_hv),
                (basis_l, basis_lv),
                (fwd_h, fwd_hv),
                (fwd_l, fwd_lv),
                (cond, cond_v),
                (cap, cap_v),
                (block_cond, bcond_v),
                (block_cap, bcap_v),
            ]
        )
    ]
    own = pltpu.make_async_copy(
        spectrum.at[:, lanes(me * nodes, nodes)], x_all.at[pl.ds(my_row, rows), :], own_sem
    )
    for copy in loads:
        copy.start()
    own.start()

    square = (n_bound, n_bound)
    diagonal = lax.broadcasted_iota(jnp.int32, square, 0) == lax.broadcasted_iota(
        jnp.int32, square, 1
    )
    spread = jnp.broadcast_to(bound[...], square)
    bound_col[...] = jnp.sum(jnp.where(diagonal, spread.astype(f32), 0.0), axis=1, keepdims=True)

    def one_hot(first, size):
        ids = (first + lax.broadcasted_iota(jnp.int32, (n_bound, size), 1)).astype(f32)
        return jnp.where(ids == bound_col[...], 1.0, 0.0).astype(bf16)

    loads[0].wait()

    def pick(i, total):
        columns = lanes(i * GATHER, GATHER)
        high, low = split(spec_v[:, columns])
        both = jnp.concatenate([high, low], axis=0)
        return total + lax.dot_general(
            both, one_hot(i * GATHER, GATHER), BOTH_LANES, preferred_element_type=f32
        )

    picked = lax.fori_loop(
        0, spectrum.shape[1] // GATHER, pick, jnp.zeros((2 * rows, n_bound), f32)
    )
    gathered[dom] = picked[:rows] + picked[rows:]
    for k in range(1, n_dom):
        pltpu.make_async_remote_copy(
            src_ref=gathered.at[dom],
            dst_ref=gathered.at[dom],
            send_sem=dom_send,
            recv_sem=dom_recv,
            device_id=(lax.rem(dom + k, n_dom), me),
            device_id_type=MESH,
        ).start()

    for copy in loads[1:]:
        copy.wait()
    own.wait()

    def work(c, carry):
        columns = lanes(c * CHUNK, CHUNK)
        arrived = x_all.at[pl.ds(0, (n_spec - 1) * rows), columns]
        pltpu.make_async_copy(arrived, arrived, go_recv.at[c]).wait()
        x = x_all[:, columns]
        wave = dot3((basis_hv[...], basis_lv[...]), split(x))
        both = jnp.concatenate([cond_v[:, columns] * wave, cap_v[:, columns] * wave], axis=0)
        y = dot3((fwd_hv[...], fwd_lv[...]), split(both))
        slope = derivative(x, 0, length)
        size = bcond_v.shape[1]
        parts = []
        for b in range(CHUNK // size):
            block = c * (CHUNK // size) + b
            here = slice(b * size, (b + 1) * size)
            pair = jnp.concatenate([x[:, here], slope[:, here]], axis=1)
            matrix = jnp.concatenate([bcond_v[block], bcap_v[block]], axis=1)
            parts.append(y[:, here] + dot3(split(pair), split(matrix), BOTH_LANES))
        y_all[:, columns] = jnp.concatenate(parts, axis=1)
        target = lanes(me * nodes + c * CHUNK, CHUNK)
        for k in range(1, n_spec):
            peer = spec_peer(k)
            pltpu.make_async_remote_copy(
                src_ref=y_all.at[pl.ds(pl.multiple_of(peer * rows, rows), rows), columns],
                dst_ref=o_all.at[:, target],
                send_sem=back_send,
                recv_sem=back_recv.at[c],
                device_id=(dom, peer),
                device_id_type=MESH,
            ).start()
        pltpu.make_async_copy(
            y_all.at[pl.ds(my_row, rows), columns], o_all.at[:, target], keep_sem.at[c]
        ).start()
        return carry

    lax.fori_loop(0, n_chunks, work, 0)

    others = gathered.at[pl.ds(0, n_dom - 1)]
    pltpu.make_async_copy(others, others, dom_recv).wait()
    total = jnp.zeros((rows, n_bound), f32)
    for c in range(sources.shape[1]):
        value = jnp.zeros((rows, n_bound), f32)
        for p in range(n_dom):
            chosen = jnp.where((sources[0, c] == p) & (c < used[0]), 1.0, 0.0)
            value = value + chosen * gathered[p]
        slope = derivative(value, me * rows, length)
        total = total + dot3(split(value), split(ccond_v[c]), BOTH_LANES)
        total = total + dot3(split(slope), split(ccap_v[c]), BOTH_LANES)
    current[...] = total

    def finish(c, carry):
        every = o_all.at[:, pl.ds(0, (n_spec - 1) * CHUNK)]
        pltpu.make_async_copy(every, every, back_recv.at[c]).wait()
        kept = o_all.at[:, pl.ds(0, CHUNK)]
        pltpu.make_async_copy(kept, kept, keep_sem.at[c]).wait()
        high, low = split(current[...])
        for s in range(n_spec):
            first = s * nodes + c * CHUNK
            columns = lanes(first, CHUNK)
            chosen = one_hot(first, CHUNK)
            o_all[:, columns] += jnp.dot(high, chosen, preferred_element_type=f32) + jnp.dot(
                low, chosen, preferred_element_type=f32
            )
            pltpu.make_async_copy(o_all.at[:, columns], out.at[:, columns], out_sem).start()
        return carry

    lax.fori_loop(0, n_chunks, finish, 0)

    pltpu.make_async_copy(o_all, out, out_sem).wait()
    sent = spectrum.at[:, pl.ds(0, (n_spec - 1) * nodes)]
    pltpu.make_async_copy(sent, sent, go_send).wait()
    sent = y_all.at[pl.ds(0, (n_spec - 1) * rows), :]
    pltpu.make_async_copy(sent, sent, back_send).wait()
    pltpu.make_async_copy(others, others, dom_send).wait()


def solution(mesh):
    n_dom, n_spec = mesh.shape["dom"], mesh.shape["spec"]

    def shards(
        spectrum,
        cond,
        cap,
        block_cond,
        block_cap,
        bound,
        sources,
        used,
        couple_cond,
        couple_cap,
    ):
        rows = spectrum.shape[0]
        length, nodes = cond.shape
        n_bound = bound.shape[1]
        n_chunks = nodes // CHUNK
        tables = [jnp.asarray(t) for t in fourier_tables(length)]
        couple_cond, couple_cap = couple_cond[0], couple_cap[0]
        anywhere = pl.BlockSpec(memory_space=pl.ANY)
        vmem = pl.BlockSpec(memory_space=pltpu.VMEM)
        smem = pl.BlockSpec(memory_space=pltpu.SMEM)
        dma = pltpu.SemaphoreType.DMA
        return pl.pallas_call(
            functools.partial(kernel, n_dom, n_spec),
            out_shape=jax.ShapeDtypeStruct(spectrum.shape, f32),
            in_specs=[anywhere] * 5 + [vmem, smem, smem] + [anywhere] * 6,
            out_specs=anywhere,
            scratch_shapes=[
                pltpu.VMEM((length, nodes), f32),
                pltpu.VMEM((length, nodes), f32),
                pltpu.VMEM(spectrum.shape, f32),
                pltpu.VMEM(spectrum.shape, f32),
                pltpu.VMEM(cond.shape, f32),
                pltpu.VMEM(cap.shape, f32),
                pltpu.VMEM(block_cond.shape, f32),
                pltpu.VMEM(block_cap.shape, f32),
                pltpu.VMEM(couple_cond.shape, f32),
                pltpu.VMEM(couple_cap.shape, f32),
            ]
            + [pltpu.VMEM(t.shape, bf16) for t in tables]
            + [
                pltpu.VMEM((n_dom, rows, n_bound), f32),
                pltpu.VMEM((n_bound, 1), f32),
                pltpu.VMEM((rows, n_bound), f32),
                dma((11,)),
                dma,
                dma((n_chunks,)),
                dma,
                dma,
                dma((n_chunks,)),
                dma,
                dma((n_chunks,)),
                dma,
                dma,
            ],
            compiler_params=pltpu.CompilerParams(
                collective_id=0, has_side_effects=True, vmem_limit_bytes=56 * 1024 * 1024
            ),
            cost_estimate=pl.CostEstimate(
                flops=6 * length * nodes * (4 * length), bytes_accessed=20 << 20, transcendentals=0
            ),
        )(
            spectrum,
            cond,
            cap,
            block_cond,
            block_cap,
            bound,
            sources,
            used,
            couple_cond,
            couple_cap,
            *tables,
        )

    return jax.shard_map(
        shards,
        mesh=mesh,
        in_specs=(
            P("spec", "dom"),
            P(None, ("dom", "spec")),
            P(None, ("dom", "spec")),
            P(("dom", "spec"), None, None),
            P(("dom", "spec"), None, None),
            P("dom", None),
            P("dom", None),
            P("dom"),
            P("dom", None, None, None),
            P("dom", None, None, None),
        ),
        out_specs=P("spec", "dom"),
        check_vma=False,
    )
```

```python
import functools
import math

import jax
import jax.numpy as jnp
import ml_dtypes
import numpy as np
from jax import lax
from jax.experimental import pallas as pl
from jax.experimental.pallas import tpu as pltpu
from jax.sharding import PartitionSpec as P

MESH = pl.DeviceIdType.MESH
CHUNK = 512
GATHER = 2048
f32 = jnp.float32
bf16 = jnp.bfloat16


def split_table(table):
    high = table.astype(ml_dtypes.bfloat16)
    low = (table - high.astype(np.float64)).astype(ml_dtypes.bfloat16)
    return high, low


def fourier_tables(length):
    ids = np.arange(length)
    harmonic = np.where(ids == 1, length // 2, ids // 2)
    phase = (ids[:, None] * harmonic[None, :]) % length
    angles = phase * (2.0 * math.pi / length)
    is_sine = (ids % 2 == 1) & (ids >= 2)
    basis = np.where(is_sine[None, :], np.sin(angles), np.cos(angles))
    forward = basis.T * np.where(ids < 2, 1.0 / length, 2.0 / length)[:, None]
    frequency = np.where(ids >= 2, (ids // 2) * (2.0 / length), 0.0)[:, None]
    swapped = forward.reshape(length // 2, 2, length)[:, ::-1].reshape(length, length)
    slope = np.where((ids % 2 == 0)[:, None], frequency, -frequency) * swapped
    return split_table(basis) + split_table(np.concatenate([forward, slope], axis=1))


def split(values):
    high = values.astype(bf16)
    return high, (values - high.astype(f32)).astype(bf16)


def dot3(left, right, dims=(((1,), (0,)), ((), ()))):
    dot = functools.partial(lax.dot_general, dimension_numbers=dims, preferred_element_type=f32)
    return dot(left[0], right[0]) + (dot(left[0], right[1]) + dot(left[1], right[0]))


BOTH_LANES = (((1,), (1,)), ((), ()))


def derivative(values, first_row, length):
    rows = values.shape[0]
    ids = first_row + lax.broadcasted_iota(jnp.int32, (rows, 1), 0)
    frequency = (ids // 2).astype(f32) * (2.0 / length)
    even = ids % 2 == 0
    from_next = jnp.where(even, frequency, 0.0)
    from_last = jnp.where(even, 0.0, -frequency)
    return from_next * pltpu.roll(values, rows - 1, 0) + from_last * pltpu.roll(values, 1, 0)


def kernel(
    n_dom,
    n_spec,
    spectrum,
    cond,
    cap,
    block_cond,
    block_cap,
    bound,
    sources,
    used,
    couple_cond,
    couple_cap,
    basis_h,
    basis_l,
    fwd_h,
    fwd_l,
    o_all,
    x_all,
    y_all,
    spec_v,
    cond_v,
    cap_v,
    bcond_v,
    bcap_v,
    ccond_v,
    ccap_v,
    basis_hv,
    basis_lv,
    fwd_hv,
    fwd_lv,
    gathered,
    bound_col,
    current,
    load_sem,
    own_sem,
    keep_sem,
    go_send,
    go_recv,
    back_send,
    back_recv,
    dom_send,
    dom_recv,
):
    rows = spectrum.shape[0]
    length, nodes = cond.shape
    n_bound = bound.shape[1]
    n_chunks = nodes // CHUNK
    dom = lax.axis_index("dom")
    me = lax.axis_index("spec")
    my_row = pl.multiple_of(me * rows, rows)

    def spec_peer(k):
        return lax.rem(me + k, n_spec)

    barrier = pltpu.get_barrier_semaphore()
    for k in range(1, n_spec):
        pl.semaphore_signal(barrier, inc=1, device_id=(dom, spec_peer(k)), device_id_type=MESH)
    for k in range(1, n_dom):
        pl.semaphore_signal(
            barrier, inc=1, device_id=(lax.rem(dom + k, n_dom), me), device_id_type=MESH
        )
    def lanes(first, size):
        return pl.ds(pl.multiple_of(first, size), size)

    loads = [
        pltpu.make_async_copy(source, target, load_sem.at[i])
        for i, (source, target) in enumerate(
            [
                (spectrum, spec_v),
                (couple_cond, ccond_v),
                (couple_cap, ccap_v),
                (basis_h, basis_hv),
                (basis_l, basis_lv),
                (fwd_h, fwd_hv),
                (fwd_l, fwd_lv),
                (cond, cond_v),
                (cap, cap_v),
                (block_cond, bcond_v),
                (block_cap, bcap_v),
            ]
        )
    ]
    own = pltpu.make_async_copy(
        spectrum.at[:, lanes(me * nodes, nodes)], x_all.at[pl.ds(my_row, rows), :], own_sem
    )
    for copy in loads:
        copy.start()
    own.start()

    pl.semaphore_wait(barrier, n_spec - 1 + n_dom - 1)

    def send_go(c, carry):
        for k in range(1, n_spec):
            peer = spec_peer(k)
            pltpu.make_async_remote_copy(
                src_ref=spectrum.at[:, lanes(peer * nodes + c * CHUNK, CHUNK)],
                dst_ref=x_all.at[pl.ds(my_row, rows), lanes(c * CHUNK, CHUNK)],
                send_sem=go_send,
                recv_sem=go_recv.at[c],
                device_id=(dom, peer),
                device_id_type=MESH,
            ).start()
        return carry

    lax.fori_loop(0, n_chunks, send_go, 0)

    square = (n_bound, n_bound)
    diagonal = lax.broadcasted_iota(jnp.int32, square, 0) == lax.broadcasted_iota(
        jnp.int32, square, 1
    )
    spread = jnp.broadcast_to(bound[...], square)
    bound_col[...] = jnp.sum(jnp.where(diagonal, spread.astype(f32), 0.0), axis=1, keepdims=True)

    def one_hot(first, size):
        ids = (first + lax.broadcasted_iota(jnp.int32, (n_bound, size), 1)).astype(f32)
        return jnp.where(ids == bound_col[...], 1.0, 0.0).astype(bf16)

    loads[0].wait()

    def pick(i, total):
        columns = lanes(i * GATHER, GATHER)
        high, low = split(spec_v[:, columns])
        both = jnp.concatenate([high, low], axis=0)
        return total + lax.dot_general(
            both, one_hot(i * GATHER, GATHER), BOTH_LANES, preferred_element_type=f32
        )

    picked = lax.fori_loop(
        0, spectrum.shape[1] // GATHER, pick, jnp.zeros((2 * rows, n_bound), f32)
    )
    gathered[dom] = picked[:rows] + picked[rows:]
    for k in range(1, n_dom):
        pltpu.make_async_remote_copy(
            src_ref=gathered.at[dom],
            dst_ref=gathered.at[dom],
            send_sem=dom_send,
            recv_sem=dom_recv,
            device_id=(lax.rem(dom + k, n_dom), me),
            device_id_type=MESH,
        ).start()

    for copy in loads[1:]:
        copy.wait()
    own.wait()

    def work(c, carry):
        columns = lanes(c * CHUNK, CHUNK)
        arrived = x_all.at[pl.ds(0, (n_spec - 1) * rows), columns]
        pltpu.make_async_copy(arrived, arrived, go_recv.at[c]).wait()
        x = x_all[:, columns]
        wave = dot3((basis_hv[...], basis_lv[...]), split(x))
        both = jnp.concatenate([cond_v[:, columns] * wave, cap_v[:, columns] * wave], axis=0)
        y = dot3((fwd_hv[...], fwd_lv[...]), split(both))
        slope = derivative(x, 0, length)
        size = bcond_v.shape[1]
        parts = []
        for b in range(CHUNK // size):
            block = c * (CHUNK // size) + b
            here = slice(b * size, (b + 1) * size)
            pair = jnp.concatenate([x[:, here], slope[:, here]], axis=1)
            matrix = jnp.concatenate([bcond_v[block], bcap_v[block]], axis=1)
            parts.append(y[:, here] + dot3(split(pair), split(matrix), BOTH_LANES))
        y_all[:, columns] = jnp.concatenate(parts, axis=1)
        target = lanes(me * nodes + c * CHUNK, CHUNK)
        for k in range(1, n_spec):
            peer = spec_peer(k)
            pltpu.make_async_remote_copy(
                src_ref=y_all.at[pl.ds(pl.multiple_of(peer * rows, rows), rows), columns],
                dst_ref=o_all.at[:, target],
                send_sem=back_send,
                recv_sem=back_recv.at[c],
                device_id=(dom, peer),
                device_id_type=MESH,
            ).start()
        pltpu.make_async_copy(
            y_all.at[pl.ds(my_row, rows), columns], o_all.at[:, target], keep_sem.at[c]
        ).start()
        return carry

    lax.fori_loop(0, n_chunks, work, 0)

    others = gathered.at[pl.ds(0, n_dom - 1)]
    pltpu.make_async_copy(others, others, dom_recv).wait()
    total = jnp.zeros((rows, n_bound), f32)
    for c in range(sources.shape[1]):
        value = jnp.zeros((rows, n_bound), f32)
        for p in range(n_dom):
            chosen = jnp.where((sources[0, c] == p) & (c < used[0]), 1.0, 0.0)
            value = value + chosen * gathered[p]
        slope = derivative(value, me * rows, length)
        total = total + dot3(split(value), split(ccond_v[c]), BOTH_LANES)
        total = total + dot3(split(slope), split(ccap_v[c]), BOTH_LANES)
    current[...] = total

    def place(i, carry):
        columns = lanes(i * GATHER, GATHER)
        high, low = split(current[...])
        chosen = one_hot(i * GATHER, GATHER)
        spec_v[:, columns] = jnp.dot(high, chosen, preferred_element_type=f32) + jnp.dot(
            low, chosen, preferred_element_type=f32
        )
        return carry

    lax.fori_loop(0, spectrum.shape[1] // GATHER, place, 0)

    def finish(c, carry):
        every = o_all.at[:, pl.ds(0, (n_spec - 1) * CHUNK)]
        pltpu.make_async_copy(every, every, back_recv.at[c]).wait()
        kept = o_all.at[:, pl.ds(0, CHUNK)]
        pltpu.make_async_copy(kept, kept, keep_sem.at[c]).wait()
        for s in range(n_spec):
            columns = lanes(s * nodes + c * CHUNK, CHUNK)
            o_all[:, columns] += spec_v[:, columns]
        return carry

    lax.fori_loop(0, n_chunks, finish, 0)

    sent = spectrum.at[:, pl.ds(0, (n_spec - 1) * nodes)]
    pltpu.make_async_copy(sent, sent, go_send).wait()
    sent = y_all.at[pl.ds(0, (n_spec - 1) * rows), :]
    pltpu.make_async_copy(sent, sent, back_send).wait()
    pltpu.make_async_copy(others, others, dom_send).wait()


def solution(mesh):
    n_dom, n_spec = mesh.shape["dom"], mesh.shape["spec"]

    def shards(
        spectrum,
        cond,
        cap,
        block_cond,
        block_cap,
        bound,
        sources,
        used,
        couple_cond,
        couple_cap,
    ):
        rows = spectrum.shape[0]
        length, nodes = cond.shape
        n_bound = bound.shape[1]
        n_chunks = nodes // CHUNK
        tables = [jnp.asarray(t) for t in fourier_tables(length)]
        couple_cond, couple_cap = couple_cond[0], couple_cap[0]
        anywhere = pl.BlockSpec(memory_space=pl.ANY)
        vmem = pl.BlockSpec(memory_space=pltpu.VMEM)
        smem = pl.BlockSpec(memory_space=pltpu.SMEM)
        dma = pltpu.SemaphoreType.DMA
        return pl.pallas_call(
            functools.partial(kernel, n_dom, n_spec),
            out_shape=pltpu.VMEM(spectrum.shape, f32),
            in_specs=[anywhere] * 5 + [vmem, smem, smem] + [anywhere] * 6,
            out_specs=vmem,
            scratch_shapes=[
                pltpu.VMEM((length, nodes), f32),
                pltpu.VMEM((length, nodes), f32),
                pltpu.VMEM(spectrum.shape, f32),
                pltpu.VMEM(cond.shape, f32),
                pltpu.VMEM(cap.shape, f32),
                pltpu.VMEM(block_cond.shape, f32),
                pltpu.VMEM(block_cap.shape, f32),
                pltpu.VMEM(couple_cond.shape, f32),
                pltpu.VMEM(couple_cap.shape, f32),
            ]
            + [pltpu.VMEM(t.shape, bf16) for t in tables]
            + [
                pltpu.VMEM((n_dom, rows, n_bound), f32),
                pltpu.VMEM((n_bound, 1), f32),
                pltpu.VMEM((rows, n_bound), f32),
                dma((11,)),
                dma,
                dma((n_chunks,)),
                dma,
                dma((n_chunks,)),
                dma,
                dma((n_chunks,)),
                dma,
                dma,
            ],
            compiler_params=pltpu.CompilerParams(
                collective_id=0, has_side_effects=True, vmem_limit_bytes=56 * 1024 * 1024
            ),
            cost_estimate=pl.CostEstimate(
                flops=6 * length * nodes * (4 * length), bytes_accessed=20 << 20, transcendentals=0
            ),
        )(
            spectrum,
            cond,
            cap,
            block_cond,
            block_cap,
            bound,
            sources,
            used,
            couple_cond,
            couple_cap,
            *tables,
        )

    return jax.shard_map(
        shards,
        mesh=mesh,
        in_specs=(
            P("spec", "dom"),
            P(None, ("dom", "spec")),
            P(None, ("dom", "spec")),
            P(("dom", "spec"), None, None),
            P(("dom", "spec"), None, None),
            P("dom", None),
            P("dom", None),
            P("dom"),
            P("dom", None, None, None),
            P("dom", None, None, None),
        ),
        out_specs=P("spec", "dom"),
        check_vma=False,
    )
```

```python
import functools
import math

import jax
import jax.numpy as jnp
import ml_dtypes
import numpy as np
from jax import lax
from jax.experimental import pallas as pl
from jax.experimental.pallas import tpu as pltpu
from jax.sharding import PartitionSpec as P

MESH = pl.DeviceIdType.MESH
CHUNK = 512
GATHER = 2048
f32 = jnp.float32
bf16 = jnp.bfloat16


def split_table(table):
    high = table.astype(ml_dtypes.bfloat16)
    low = (table - high.astype(np.float64)).astype(ml_dtypes.bfloat16)
    return high, low


def fourier_tables(length):
    ids = np.arange(length)
    harmonic = np.where(ids == 1, length // 2, ids // 2)
    phase = (ids[:, None] * harmonic[None, :]) % length
    angles = phase * (2.0 * math.pi / length)
    is_sine = (ids % 2 == 1) & (ids >= 2)
    basis = np.where(is_sine[None, :], np.sin(angles), np.cos(angles))
    forward = basis.T * np.where(ids < 2, 1.0 / length, 2.0 / length)[:, None]
    frequency = np.where(ids >= 2, (ids // 2) * (2.0 / length), 0.0)[:, None]
    swapped = forward.reshape(length // 2, 2, length)[:, ::-1].reshape(length, length)
    slope = np.where((ids % 2 == 0)[:, None], frequency, -frequency) * swapped
    return split_table(basis) + split_table(np.concatenate([forward, slope], axis=1))


def split(values):
    high = values.astype(bf16)
    return high, (values - high.astype(f32)).astype(bf16)


def dot3(left, right, dims=(((1,), (0,)), ((), ()))):
    dot = functools.partial(lax.dot_general, dimension_numbers=dims, preferred_element_type=f32)
    return dot(left[0], right[0]) + (dot(left[0], right[1]) + dot(left[1], right[0]))


BOTH_LANES = (((1,), (1,)), ((), ()))


def derivative(values, first_row, length):
    rows = values.shape[0]
    ids = first_row + lax.broadcasted_iota(jnp.int32, (rows, 1), 0)
    frequency = (ids // 2).astype(f32) * (2.0 / length)
    even = ids % 2 == 0
    from_next = jnp.where(even, frequency, 0.0)
    from_last = jnp.where(even, 0.0, -frequency)
    return from_next * pltpu.roll(values, rows - 1, 0) + from_last * pltpu.roll(values, 1, 0)


def kernel(
    n_dom,
    n_spec,
    spectrum,
    cond,
    cap,
    block_cond,
    block_cap,
    bound,
    sources,
    used,
    couple_cond,
    couple_cap,
    basis_h,
    basis_l,
    fwd_h,
    fwd_l,
    o_all,
    x_all,
    y_all,
    spec_v,
    cond_v,
    cap_v,
    bcond_v,
    bcap_v,
    ccond_v,
    ccap_v,
    basis_hv,
    basis_lv,
    fwd_hv,
    fwd_lv,
    gathered,
    bound_col,
    current,
    load_sem,
    own_sem,
    keep_sem,
    go_send,
    go_recv,
    back_send,
    back_recv,
    dom_send,
    dom_recv,
):
    rows = spectrum.shape[0]
    length, nodes = cond.shape
    n_bound = bound.shape[1]
    n_chunks = nodes // CHUNK
    dom = lax.axis_index("dom")
    me = lax.axis_index("spec")
    my_row = pl.multiple_of(me * rows, rows)

    def spec_peer(k):
        return lax.rem(me + k, n_spec)

    half = n_spec // 2
    side, place_in_half = me // half, lax.rem(me, half)
    far = [(1 - side) * half + lax.rem(place_in_half + i, half) for i in range(half)]
    near = [side * half + lax.rem(place_in_half + i, half) for i in range(1, half)]
    mixed = [far[0]]
    for one, other in zip(near, far[1:]):
        mixed += [one, other]

    barrier = pltpu.get_barrier_semaphore()
    for k in range(1, n_spec):
        pl.semaphore_signal(barrier, inc=1, device_id=(dom, spec_peer(k)), device_id_type=MESH)
    for k in range(1, n_dom):
        pl.semaphore_signal(
            barrier, inc=1, device_id=(lax.rem(dom + k, n_dom), me), device_id_type=MESH
        )
    def lanes(first, size):
        return pl.ds(pl.multiple_of(first, size), size)

    loads = [
        pltpu.make_async_copy(source, target, load_sem.at[i])
        for i, (source, target) in enumerate(
            [
                (spectrum, spec_v),
                (couple_cond, ccond_v),
                (couple_cap, ccap_v),
                (basis_h, basis_hv),
                (basis_l, basis_lv),
                (fwd_h, fwd_hv),
                (fwd_l, fwd_lv),
                (cond, cond_v),
                (cap, cap_v),
                (block_cond, bcond_v),
                (block_cap, bcap_v),
            ]
        )
    ]
    own = pltpu.make_async_copy(
        spectrum.at[:, lanes(me * nodes, nodes)], x_all.at[pl.ds(my_row, rows), :], own_sem
    )
    for copy in loads:
        copy.start()
    own.start()

    pl.semaphore_wait(barrier, n_spec - 1 + n_dom - 1)

    def send_go(peer, c):
        pltpu.make_async_remote_copy(
            src_ref=spectrum.at[:, lanes(peer * nodes + c * CHUNK, CHUNK)],
            dst_ref=x_all.at[pl.ds(my_row, rows), lanes(c * CHUNK, CHUNK)],
            send_sem=go_send,
            recv_sem=go_recv.at[c],
            device_id=(dom, peer),
            device_id_type=MESH,
        ).start()

    for peer in far:
        send_go(peer, 0)

    def send_both(c, carry):
        send_go(far[0], c + 1)
        for one, other in zip(near, far[1:]):
            send_go(one, c)
            send_go(other, c + 1)
        return carry

    lax.fori_loop(0, n_chunks - 1, send_both, 0)
    for peer in near:
        send_go(peer, n_chunks - 1)

    square = (n_bound, n_bound)
    diagonal = lax.broadcasted_iota(jnp.int32, square, 0) == lax.broadcasted_iota(
        jnp.int32, square, 1
    )
    spread = jnp.broadcast_to(bound[...], square)
    bound_col[...] = jnp.sum(jnp.where(diagonal, spread.astype(f32), 0.0), axis=1, keepdims=True)

    def one_hot(first, size):
        ids = (first + lax.broadcasted_iota(jnp.int32, (n_bound, size), 1)).astype(f32)
        return jnp.where(ids == bound_col[...], 1.0, 0.0).astype(bf16)

    loads[0].wait()

    def pick(i, total):
        columns = lanes(i * GATHER, GATHER)
        high, low = split(spec_v[:, columns])
        both = jnp.concatenate([high, low], axis=0)
        return total + lax.dot_general(
            both, one_hot(i * GATHER, GATHER), BOTH_LANES, preferred_element_type=f32
        )

    picked = lax.fori_loop(
        0, spectrum.shape[1] // GATHER, pick, jnp.zeros((2 * rows, n_bound), f32)
    )
    gathered[dom] = picked[:rows] + picked[rows:]
    for k in range(1, n_dom):
        pltpu.make_async_remote_copy(
            src_ref=gathered.at[dom],
            dst_ref=gathered.at[dom],
            send_sem=dom_send,
            recv_sem=dom_recv,
            device_id=(lax.rem(dom + k, n_dom), me),
            device_id_type=MESH,
        ).start()

    for copy in loads[1:]:
        copy.wait()
    own.wait()

    def work(c, carry):
        columns = lanes(c * CHUNK, CHUNK)
        arrived = x_all.at[pl.ds(0, (n_spec - 1) * rows), columns]
        pltpu.make_async_copy(arrived, arrived, go_recv.at[c]).wait()
        x = x_all[:, columns]
        wave = dot3((basis_hv[...], basis_lv[...]), split(x))
        both = jnp.concatenate([cond_v[:, columns] * wave, cap_v[:, columns] * wave], axis=0)
        y = dot3((fwd_hv[...], fwd_lv[...]), split(both))
        slope = derivative(x, 0, length)
        size = bcond_v.shape[1]
        parts = []
        for b in range(CHUNK // size):
            block = c * (CHUNK // size) + b
            here = slice(b * size, (b + 1) * size)
            pair = jnp.concatenate([x[:, here], slope[:, here]], axis=1)
            matrix = jnp.concatenate([bcond_v[block], bcap_v[block]], axis=1)
            parts.append(y[:, here] + dot3(split(pair), split(matrix), BOTH_LANES))
        y_all[:, columns] = jnp.concatenate(parts, axis=1)
        target = lanes(me * nodes + c * CHUNK, CHUNK)
        for peer in mixed:
            pltpu.make_async_remote_copy(
                src_ref=y_all.at[pl.ds(pl.multiple_of(peer * rows, rows), rows), columns],
                dst_ref=o_all.at[:, target],
                send_sem=back_send,
                recv_sem=back_recv.at[c],
                device_id=(dom, peer),
                device_id_type=MESH,
            ).start()
        pltpu.make_async_copy(
            y_all.at[pl.ds(my_row, rows), columns], o_all.at[:, target], keep_sem.at[c]
        ).start()
        return carry

    lax.fori_loop(0, n_chunks, work, 0)

    others = gathered.at[pl.ds(0, n_dom - 1)]
    pltpu.make_async_copy(others, others, dom_recv).wait()
    total = jnp.zeros((rows, n_bound), f32)
    for c in range(sources.shape[1]):
        value = jnp.zeros((rows, n_bound), f32)
        for p in range(n_dom):
            chosen = jnp.where((sources[0, c] == p) & (c < used[0]), 1.0, 0.0)
            value = value + chosen * gathered[p]
        slope = derivative(value, me * rows, length)
        total = total + dot3(split(value), split(ccond_v[c]), BOTH_LANES)
        total = total + dot3(split(slope), split(ccap_v[c]), BOTH_LANES)
    current[...] = total

    def place(i, carry):
        columns = lanes(i * GATHER, GATHER)
        high, low = split(current[...])
        chosen = one_hot(i * GATHER, GATHER)
        spec_v[:, columns] = jnp.dot(high, chosen, preferred_element_type=f32) + jnp.dot(
            low, chosen, preferred_element_type=f32
        )
        return carry

    lax.fori_loop(0, spectrum.shape[1] // GATHER, place, 0)

    def finish(c, carry):
        every = o_all.at[:, pl.ds(0, (n_spec - 1) * CHUNK)]
        pltpu.make_async_copy(every, every, back_recv.at[c]).wait()
        kept = o_all.at[:, pl.ds(0, CHUNK)]
        pltpu.make_async_copy(kept, kept, keep_sem.at[c]).wait()
        for s in range(n_spec):
            columns = lanes(s * nodes + c * CHUNK, CHUNK)
            o_all[:, columns] += spec_v[:, columns]
        return carry

    lax.fori_loop(0, n_chunks, finish, 0)

    sent = spectrum.at[:, pl.ds(0, (n_spec - 1) * nodes)]
    pltpu.make_async_copy(sent, sent, go_send).wait()
    sent = y_all.at[pl.ds(0, (n_spec - 1) * rows), :]
    pltpu.make_async_copy(sent, sent, back_send).wait()
    pltpu.make_async_copy(others, others, dom_send).wait()


def solution(mesh):
    n_dom, n_spec = mesh.shape["dom"], mesh.shape["spec"]

    def shards(
        spectrum,
        cond,
        cap,
        block_cond,
        block_cap,
        bound,
        sources,
        used,
        couple_cond,
        couple_cap,
    ):
        rows = spectrum.shape[0]
        length, nodes = cond.shape
        n_bound = bound.shape[1]
        n_chunks = nodes // CHUNK
        tables = [jnp.asarray(t) for t in fourier_tables(length)]
        couple_cond, couple_cap = couple_cond[0], couple_cap[0]
        anywhere = pl.BlockSpec(memory_space=pl.ANY)
        vmem = pl.BlockSpec(memory_space=pltpu.VMEM)
        smem = pl.BlockSpec(memory_space=pltpu.SMEM)
        dma = pltpu.SemaphoreType.DMA
        return pl.pallas_call(
            functools.partial(kernel, n_dom, n_spec),
            out_shape=pltpu.VMEM(spectrum.shape, f32),
            in_specs=[anywhere] * 5 + [vmem, smem, smem] + [anywhere] * 6,
            out_specs=vmem,
            scratch_shapes=[
                pltpu.VMEM((length, nodes), f32),
                pltpu.VMEM((length, nodes), f32),
                pltpu.VMEM(spectrum.shape, f32),
                pltpu.VMEM(cond.shape, f32),
                pltpu.VMEM(cap.shape, f32),
                pltpu.VMEM(block_cond.shape, f32),
                pltpu.VMEM(block_cap.shape, f32),
                pltpu.VMEM(couple_cond.shape, f32),
                pltpu.VMEM(couple_cap.shape, f32),
            ]
            + [pltpu.VMEM(t.shape, bf16) for t in tables]
            + [
                pltpu.VMEM((n_dom, rows, n_bound), f32),
                pltpu.VMEM((n_bound, 1), f32),
                pltpu.VMEM((rows, n_bound), f32),
                dma((11,)),
                dma,
                dma((n_chunks,)),
                dma,
                dma((n_chunks,)),
                dma,
                dma((n_chunks,)),
                dma,
                dma,
            ],
            compiler_params=pltpu.CompilerParams(
                collective_id=0, has_side_effects=True, vmem_limit_bytes=56 * 1024 * 1024
            ),
            cost_estimate=pl.CostEstimate(
                flops=6 * length * nodes * (4 * length), bytes_accessed=20 << 20, transcendentals=0
            ),
        )(
            spectrum,
            cond,
            cap,
            block_cond,
            block_cap,
            bound,
            sources,
            used,
            couple_cond,
            couple_cap,
            *tables,
        )

    return jax.shard_map(
        shards,
        mesh=mesh,
        in_specs=(
            P("spec", "dom"),
            P(None, ("dom", "spec")),
            P(None, ("dom", "spec")),
            P(("dom", "spec"), None, None),
            P(("dom", "spec"), None, None),
            P("dom", None),
            P("dom", None),
            P("dom"),
            P("dom", None, None, None),
            P("dom", None, None, None),
        ),
        out_specs=P("spec", "dom"),
        check_vma=False,
    )
```

```python
import functools
import math

import jax
import jax.numpy as jnp
import numpy as np
from jax import lax
from jax.experimental import pallas as pl
from jax.experimental.pallas import tpu as pltpu
from jax.sharding import PartitionSpec as P

MESH = pl.DeviceIdType.MESH
CHUNK = 512
AHEAD = 3
GATHER = 2048
f32 = jnp.float32
bf16 = jnp.bfloat16


def fourier_tables(length):
    ids = np.arange(length)
    harmonic = np.where(ids == 1, length // 2, ids // 2)
    phase = (ids[:, None] * harmonic[None, :]) % length
    angles = phase * (2.0 * math.pi / length)
    is_sine = (ids % 2 == 1) & (ids >= 2)
    basis = np.where(is_sine[None, :], np.sin(angles), np.cos(angles))
    forward = basis.T * np.where(ids < 2, 1.0 / length, 2.0 / length)[:, None]
    frequency = np.where(ids >= 2, (ids // 2) * (2.0 / length), 0.0)[:, None]
    swapped = forward.reshape(length // 2, 2, length)[:, ::-1].reshape(length, length)
    slope = np.where((ids % 2 == 0)[:, None], frequency, -frequency) * swapped
    both = np.concatenate([forward, slope], axis=1)
    return basis.astype(np.float32), both.astype(np.float32)


def split(values):
    high = values.astype(bf16)
    return high, (values - high.astype(f32)).astype(bf16)


def dot3(left, right, dims=(((1,), (0,)), ((), ()))):
    dot = functools.partial(lax.dot_general, dimension_numbers=dims, preferred_element_type=f32)
    return dot(left[0], right[0]) + (dot(left[0], right[1]) + dot(left[1], right[0]))


BOTH_LANES = (((1,), (1,)), ((), ()))


def derivative(values, first_row, length):
    rows = values.shape[0]
    ids = first_row + lax.broadcasted_iota(jnp.int32, (rows, 1), 0)
    frequency = (ids // 2).astype(f32) * (2.0 / length)
    even = ids % 2 == 0
    from_next = jnp.where(even, frequency, 0.0)
    from_last = jnp.where(even, 0.0, -frequency)
    return from_next * pltpu.roll(values, rows - 1, 0) + from_last * pltpu.roll(values, 1, 0)


def kernel(
    n_dom,
    n_spec,
    spectrum,
    cond,
    cap,
    block_cond,
    block_cap,
    bound,
    sources,
    used,
    couple_cond,
    couple_cap,
    basis,
    forward,
    o_all,
    x_all,
    y_all,
    spec_v,
    cond_v,
    cap_v,
    bcond_v,
    bcap_v,
    ccond_v,
    ccap_v,
    basis_v,
    forward_v,
    basis_hv,
    basis_lv,
    fwd_hv,
    fwd_lv,
    gathered,
    bound_col,
    current,
    load_sem,
    own_sem,
    keep_sem,
    go_send,
    go_recv,
    back_send,
    back_recv,
    dom_send,
    dom_recv,
):
    rows = spectrum.shape[0]
    length, nodes = cond.shape
    n_bound = bound.shape[1]
    n_chunks = nodes // CHUNK
    dom = lax.axis_index("dom")
    me = lax.axis_index("spec")
    my_row = pl.multiple_of(me * rows, rows)

    def spec_peer(k):
        return lax.rem(me + k, n_spec)

    barrier = pltpu.get_barrier_semaphore()
    for k in range(1, n_spec):
        pl.semaphore_signal(barrier, inc=1, device_id=(dom, spec_peer(k)), device_id_type=MESH)
    for k in range(1, n_dom):
        pl.semaphore_signal(
            barrier, inc=1, device_id=(lax.rem(dom + k, n_dom), me), device_id_type=MESH
        )
    def lanes(first, size):
        return pl.ds(pl.multiple_of(first, size), size)

    loads = [
        pltpu.make_async_copy(source, target, load_sem.at[i])
        for i, (source, target) in enumerate(
            [
                (spectrum, spec_v),
                (couple_cond, ccond_v),
                (couple_cap, ccap_v),
                (basis, basis_v),
                (forward, forward_v),
                (cond, cond_v),
                (cap, cap_v),
                (block_cond, bcond_v),
                (block_cap, bcap_v),
            ]
        )
    ]
    own = pltpu.make_async_copy(
        spectrum.at[:, lanes(me * nodes, nodes)], x_all.at[pl.ds(my_row, rows), :], own_sem
    )
    for copy in loads:
        copy.start()
    own.start()

    pl.semaphore_wait(barrier, n_spec - 1 + n_dom - 1)

    def send_go(c, carry):
        for k in range(1, n_spec):
            peer = spec_peer(k)
            pltpu.make_async_remote_copy(
                src_ref=spectrum.at[:, lanes(peer * nodes + c * CHUNK, CHUNK)],
                dst_ref=x_all.at[pl.ds(my_row, rows), lanes(c * CHUNK, CHUNK)],
                send_sem=go_send,
                recv_sem=go_recv.at[c],
                device_id=(dom, peer),
                device_id_type=MESH,
            ).start()
        return carry

    ahead = min(AHEAD, n_chunks)
    lax.fori_loop(0, ahead, send_go, 0)

    square = (n_bound, n_bound)
    diagonal = lax.broadcasted_iota(jnp.int32, square, 0) == lax.broadcasted_iota(
        jnp.int32, square, 1
    )
    spread = jnp.broadcast_to(bound[...], square)
    bound_col[...] = jnp.sum(jnp.where(diagonal, spread.astype(f32), 0.0), axis=1, keepdims=True)

    def one_hot(first, size):
        ids = (first + lax.broadcasted_iota(jnp.int32, (n_bound, size), 1)).astype(f32)
        return jnp.where(ids == bound_col[...], 1.0, 0.0).astype(bf16)

    loads[0].wait()

    def pick(i, total):
        columns = lanes(i * GATHER, GATHER)
        high, low = split(spec_v[:, columns])
        both = jnp.concatenate([high, low], axis=0)
        return total + lax.dot_general(
            both, one_hot(i * GATHER, GATHER), BOTH_LANES, preferred_element_type=f32
        )

    picked = lax.fori_loop(
        0, spectrum.shape[1] // GATHER, pick, jnp.zeros((2 * rows, n_bound), f32)
    )
    gathered[dom] = picked[:rows] + picked[rows:]
    for k in range(1, n_dom):
        pltpu.make_async_remote_copy(
            src_ref=gathered.at[dom],
            dst_ref=gathered.at[dom],
            send_sem=dom_send,
            recv_sem=dom_recv,
            device_id=(lax.rem(dom + k, n_dom), me),
            device_id_type=MESH,
        ).start()

    for copy in loads[1:]:
        copy.wait()
    own.wait()
    basis_hv[...], basis_lv[...] = split(basis_v[...])
    fwd_hv[...], fwd_lv[...] = split(forward_v[...])

    def work(c, carry):
        columns = lanes(c * CHUNK, CHUNK)
        arrived = x_all.at[pl.ds(0, (n_spec - 1) * rows), columns]
        pltpu.make_async_copy(arrived, arrived, go_recv.at[c]).wait()

        @pl.when(c + ahead < n_chunks)
        def _():
            send_go(c + ahead, 0)

        x = x_all[:, columns]
        wave = dot3((basis_hv[...], basis_lv[...]), split(x))
        both = jnp.concatenate([cond_v[:, columns] * wave, cap_v[:, columns] * wave], axis=0)
        y = dot3((fwd_hv[...], fwd_lv[...]), split(both))
        slope = derivative(x, 0, length)
        size = bcond_v.shape[1]
        parts = []
        for b in range(CHUNK // size):
            block = c * (CHUNK // size) + b
            here = slice(b * size, (b + 1) * size)
            pair = jnp.concatenate([x[:, here], slope[:, here]], axis=1)
            matrix = jnp.concatenate([bcond_v[block], bcap_v[block]], axis=1)
            parts.append(y[:, here] + dot3(split(pair), split(matrix), BOTH_LANES))
        y_all[:, columns] = jnp.concatenate(parts, axis=1)
        target = lanes(me * nodes + c * CHUNK, CHUNK)
        for k in range(1, n_spec):
            peer = spec_peer(k)
            pltpu.make_async_remote_copy(
                src_ref=y_all.at[pl.ds(pl.multiple_of(peer * rows, rows), rows), columns],
                dst_ref=o_all.at[:, target],
                send_sem=back_send,
                recv_sem=back_recv.at[c],
                device_id=(dom, peer),
                device_id_type=MESH,
            ).start()
        pltpu.make_async_copy(
            y_all.at[pl.ds(my_row, rows), columns], o_all.at[:, target], keep_sem.at[c]
        ).start()
        return carry

    lax.fori_loop(0, n_chunks, work, 0)

    others = gathered.at[pl.ds(0, n_dom - 1)]
    pltpu.make_async_copy(others, others, dom_recv).wait()
    total = jnp.zeros((rows, n_bound), f32)
    for c in range(sources.shape[1]):
        value = jnp.zeros((rows, n_bound), f32)
        for p in range(n_dom):
            chosen = jnp.where((sources[0, c] == p) & (c < used[0]), 1.0, 0.0)
            value = value + chosen * gathered[p]
        slope = derivative(value, me * rows, length)
        total = total + dot3(split(value), split(ccond_v[c]), BOTH_LANES)
        total = total + dot3(split(slope), split(ccap_v[c]), BOTH_LANES)
    current[...] = total

    def place(i, carry):
        columns = lanes(i * GATHER, GATHER)
        high, low = split(current[...])
        chosen = one_hot(i * GATHER, GATHER)
        spec_v[:, columns] = jnp.dot(high, chosen, preferred_element_type=f32) + jnp.dot(
            low, chosen, preferred_element_type=f32
        )
        return carry

    lax.fori_loop(0, spectrum.shape[1] // GATHER, place, 0)

    def finish(c, carry):
        every = o_all.at[:, pl.ds(0, (n_spec - 1) * CHUNK)]
        pltpu.make_async_copy(every, every, back_recv.at[c]).wait()
        kept = o_all.at[:, pl.ds(0, CHUNK)]
        pltpu.make_async_copy(kept, kept, keep_sem.at[c]).wait()
        for s in range(n_spec):
            columns = lanes(s * nodes + c * CHUNK, CHUNK)
            o_all[:, columns] += spec_v[:, columns]
        return carry

    lax.fori_loop(0, n_chunks, finish, 0)

    sent = spectrum.at[:, pl.ds(0, (n_spec - 1) * nodes)]
    pltpu.make_async_copy(sent, sent, go_send).wait()
    sent = y_all.at[pl.ds(0, (n_spec - 1) * rows), :]
    pltpu.make_async_copy(sent, sent, back_send).wait()
    pltpu.make_async_copy(others, others, dom_send).wait()


def solution(mesh):
    n_dom, n_spec = mesh.shape["dom"], mesh.shape["spec"]

    def shards(
        spectrum,
        cond,
        cap,
        block_cond,
        block_cap,
        bound,
        sources,
        used,
        couple_cond,
        couple_cap,
    ):
        rows = spectrum.shape[0]
        length, nodes = cond.shape
        n_bound = bound.shape[1]
        n_chunks = nodes // CHUNK
        tables = [jnp.asarray(t) for t in fourier_tables(length)]
        couple_cond, couple_cap = couple_cond[0], couple_cap[0]
        anywhere = pl.BlockSpec(memory_space=pl.ANY)
        vmem = pl.BlockSpec(memory_space=pltpu.VMEM)
        smem = pl.BlockSpec(memory_space=pltpu.SMEM)
        dma = pltpu.SemaphoreType.DMA
        return pl.pallas_call(
            functools.partial(kernel, n_dom, n_spec),
            out_shape=pltpu.VMEM(spectrum.shape, f32),
            in_specs=[anywhere] * 5 + [vmem, smem, smem] + [anywhere] * 4,
            out_specs=vmem,
            scratch_shapes=[
                pltpu.VMEM((length, nodes), f32),
                pltpu.VMEM((length, nodes), f32),
                pltpu.VMEM(spectrum.shape, f32),
                pltpu.VMEM(cond.shape, f32),
                pltpu.VMEM(cap.shape, f32),
                pltpu.VMEM(block_cond.shape, f32),
                pltpu.VMEM(block_cap.shape, f32),
                pltpu.VMEM(couple_cond.shape, f32),
                pltpu.VMEM(couple_cap.shape, f32),
            ]
            + [pltpu.VMEM(t.shape, f32) for t in tables]
            + [pltpu.VMEM(t.shape, bf16) for t in tables for _ in range(2)]
            + [
                pltpu.VMEM((n_dom, rows, n_bound), f32),
                pltpu.VMEM((n_bound, 1), f32),
                pltpu.VMEM((rows, n_bound), f32),
                dma((9,)),
                dma,
                dma((n_chunks,)),
                dma,
                dma((n_chunks,)),
                dma,
                dma((n_chunks,)),
                dma,
                dma,
            ],
            compiler_params=pltpu.CompilerParams(
                collective_id=0, has_side_effects=True, vmem_limit_bytes=56 * 1024 * 1024
            ),
            cost_estimate=pl.CostEstimate(
                flops=6 * length * nodes * (4 * length), bytes_accessed=20 << 20, transcendentals=0
            ),
        )(
            spectrum,
            cond,
            cap,
            block_cond,
            block_cap,
            bound,
            sources,
            used,
            couple_cond,
            couple_cap,
            *tables,
        )

    return jax.shard_map(
        shards,
        mesh=mesh,
        in_specs=(
            P("spec", "dom"),
            P(None, ("dom", "spec")),
            P(None, ("dom", "spec")),
            P(("dom", "spec"), None, None),
            P(("dom", "spec"), None, None),
            P("dom", None),
            P("dom", None),
            P("dom"),
            P("dom", None, None, None),
            P("dom", None, None, None),
        ),
        out_specs=P("spec", "dom"),
        check_vma=False,
    )
```

```python
import functools
import math

import jax
import jax.numpy as jnp
import numpy as np
from jax import lax
from jax.experimental import pallas as pl
from jax.experimental.pallas import tpu as pltpu
from jax.sharding import PartitionSpec as P

MESH = pl.DeviceIdType.MESH
CHUNK = 1024
AHEAD = 4
GATHER = 2048
f32 = jnp.float32
bf16 = jnp.bfloat16


def fourier_tables(length):
    ids = np.arange(length)
    harmonic = np.where(ids == 1, length // 2, ids // 2)
    phase = (ids[:, None] * harmonic[None, :]) % length
    angles = phase * (2.0 * math.pi / length)
    is_sine = (ids % 2 == 1) & (ids >= 2)
    basis = np.where(is_sine[None, :], np.sin(angles), np.cos(angles))
    forward = basis.T * np.where(ids < 2, 1.0 / length, 2.0 / length)[:, None]
    frequency = np.where(ids >= 2, (ids // 2) * (2.0 / length), 0.0)[:, None]
    swapped = forward.reshape(length // 2, 2, length)[:, ::-1].reshape(length, length)
    slope = np.where((ids % 2 == 0)[:, None], frequency, -frequency) * swapped
    both = np.concatenate([forward, slope], axis=1)
    return basis.astype(np.float32), both.astype(np.float32)


def split(values):
    high = values.astype(bf16)
    return high, (values - high.astype(f32)).astype(bf16)


def dot3(left, right, dims=(((1,), (0,)), ((), ()))):
    dot = functools.partial(lax.dot_general, dimension_numbers=dims, preferred_element_type=f32)
    return dot(left[0], right[0]) + (dot(left[0], right[1]) + dot(left[1], right[0]))


BOTH_LANES = (((1,), (1,)), ((), ()))


def derivative(values, first_row, length):
    rows = values.shape[0]
    ids = first_row + lax.broadcasted_iota(jnp.int32, (rows, 1), 0)
    frequency = (ids // 2).astype(f32) * (2.0 / length)
    even = ids % 2 == 0
    from_next = jnp.where(even, frequency, 0.0)
    from_last = jnp.where(even, 0.0, -frequency)
    return from_next * pltpu.roll(values, rows - 1, 0) + from_last * pltpu.roll(values, 1, 0)


def kernel(
    n_dom,
    n_spec,
    spectrum,
    cond,
    cap,
    block_cond,
    block_cap,
    bound,
    sources,
    used,
    couple_cond,
    couple_cap,
    basis,
    forward,
    o_all,
    x_all,
    y_all,
    spec_v,
    cond_v,
    cap_v,
    bcond_v,
    bcap_v,
    ccond_v,
    ccap_v,
    basis_v,
    forward_v,
    basis_hv,
    basis_lv,
    fwd_hv,
    fwd_lv,
    gathered,
    bound_col,
    current,
    load_sem,
    own_sem,
    keep_sem,
    go_send,
    go_recv,
    back_send,
    back_recv,
    dom_send,
    dom_recv,
):
    rows = spectrum.shape[0]
    length, nodes = cond.shape
    n_bound = bound.shape[1]
    n_chunks = nodes // CHUNK
    dom = lax.axis_index("dom")
    me = lax.axis_index("spec")
    my_row = pl.multiple_of(me * rows, rows)

    def spec_peer(k):
        return lax.rem(me + k, n_spec)

    barrier = pltpu.get_barrier_semaphore()
    for k in range(1, n_spec):
        pl.semaphore_signal(barrier, inc=1, device_id=(dom, spec_peer(k)), device_id_type=MESH)
    for k in range(1, n_dom):
        pl.semaphore_signal(
            barrier, inc=1, device_id=(lax.rem(dom + k, n_dom), me), device_id_type=MESH
        )
    def lanes(first, size):
        return pl.ds(pl.multiple_of(first, size), size)

    loads = [
        pltpu.make_async_copy(source, target, load_sem.at[i])
        for i, (source, target) in enumerate(
            [
                (spectrum, spec_v),
                (couple_cond, ccond_v),
                (couple_cap, ccap_v),
                (basis, basis_v),
                (forward, forward_v),
                (cond, cond_v),
                (cap, cap_v),
                (block_cond, bcond_v),
                (block_cap, bcap_v),
            ]
        )
    ]
    own = pltpu.make_async_copy(
        spectrum.at[:, lanes(me * nodes, nodes)], x_all.at[pl.ds(my_row, rows), :], own_sem
    )
    for copy in loads:
        copy.start()
    own.start()

    pl.semaphore_wait(barrier, n_spec - 1 + n_dom - 1)

    def send_go(c, carry):
        for k in range(1, n_spec):
            peer = spec_peer(k)
            pltpu.make_async_remote_copy(
                src_ref=spectrum.at[:, lanes(peer * nodes + c * CHUNK, CHUNK)],
                dst_ref=x_all.at[pl.ds(my_row, rows), lanes(c * CHUNK, CHUNK)],
                send_sem=go_send,
                recv_sem=go_recv.at[c],
                device_id=(dom, peer),
                device_id_type=MESH,
            ).start()
        return carry

    ahead = min(AHEAD, n_chunks)
    lax.fori_loop(0, ahead, send_go, 0)

    square = (n_bound, n_bound)
    diagonal = lax.broadcasted_iota(jnp.int32, square, 0) == lax.broadcasted_iota(
        jnp.int32, square, 1
    )
    spread = jnp.broadcast_to(bound[...], square)
    bound_col[...] = jnp.sum(jnp.where(diagonal, spread.astype(f32), 0.0), axis=1, keepdims=True)

    def one_hot(first, size):
        ids = (first + lax.broadcasted_iota(jnp.int32, (n_bound, size), 1)).astype(f32)
        return jnp.where(ids == bound_col[...], 1.0, 0.0).astype(bf16)

    loads[0].wait()

    def pick(i, total):
        columns = lanes(i * GATHER, GATHER)
        high, low = split(spec_v[:, columns])
        both = jnp.concatenate([high, low], axis=0)
        return total + lax.dot_general(
            both, one_hot(i * GATHER, GATHER), BOTH_LANES, preferred_element_type=f32
        )

    picked = lax.fori_loop(
        0, spectrum.shape[1] // GATHER, pick, jnp.zeros((2 * rows, n_bound), f32)
    )
    gathered[dom] = picked[:rows] + picked[rows:]
    for k in range(1, n_dom):
        pltpu.make_async_remote_copy(
            src_ref=gathered.at[dom],
            dst_ref=gathered.at[dom],
            send_sem=dom_send,
            recv_sem=dom_recv,
            device_id=(lax.rem(dom + k, n_dom), me),
            device_id_type=MESH,
        ).start()

    for copy in loads[1:]:
        copy.wait()
    own.wait()
    basis_hv[...], basis_lv[...] = split(basis_v[...])
    fwd_hv[...], fwd_lv[...] = split(forward_v[...])

    def work(c, carry):
        columns = lanes(c * CHUNK, CHUNK)
        arrived = x_all.at[pl.ds(0, (n_spec - 1) * rows), columns]
        pltpu.make_async_copy(arrived, arrived, go_recv.at[c]).wait()

        @pl.when(c + ahead < n_chunks)
        def _():
            send_go(c + ahead, 0)

        x = x_all[:, columns]
        wave = dot3((basis_hv[...], basis_lv[...]), split(x))
        both = jnp.concatenate([cond_v[:, columns] * wave, cap_v[:, columns] * wave], axis=0)
        y = dot3((fwd_hv[...], fwd_lv[...]), split(both))
        slope = derivative(x, 0, length)
        size = bcond_v.shape[1]
        parts = []
        for b in range(CHUNK // size):
            block = c * (CHUNK // size) + b
            here = slice(b * size, (b + 1) * size)
            pair = jnp.concatenate([x[:, here], slope[:, here]], axis=1)
            matrix = jnp.concatenate([bcond_v[block], bcap_v[block]], axis=1)
            parts.append(y[:, here] + dot3(split(pair), split(matrix), BOTH_LANES))
        y_all[:, columns] = jnp.concatenate(parts, axis=1)
        target = lanes(me * nodes + c * CHUNK, CHUNK)
        for k in range(1, n_spec):
            peer = spec_peer(k)
            pltpu.make_async_remote_copy(
                src_ref=y_all.at[pl.ds(pl.multiple_of(peer * rows, rows), rows), columns],
                dst_ref=o_all.at[:, target],
                send_sem=back_send,
                recv_sem=back_recv.at[c],
                device_id=(dom, peer),
                device_id_type=MESH,
            ).start()
        pltpu.make_async_copy(
            y_all.at[pl.ds(my_row, rows), columns], o_all.at[:, target], keep_sem.at[c]
        ).start()
        return carry

    lax.fori_loop(0, n_chunks, work, 0)

    others = gathered.at[pl.ds(0, n_dom - 1)]
    pltpu.make_async_copy(others, others, dom_recv).wait()
    total = jnp.zeros((rows, n_bound), f32)
    for c in range(sources.shape[1]):
        value = jnp.zeros((rows, n_bound), f32)
        for p in range(n_dom):
            chosen = jnp.where((sources[0, c] == p) & (c < used[0]), 1.0, 0.0)
            value = value + chosen * gathered[p]
        slope = derivative(value, me * rows, length)
        total = total + dot3(split(value), split(ccond_v[c]), BOTH_LANES)
        total = total + dot3(split(slope), split(ccap_v[c]), BOTH_LANES)
    current[...] = total

    def place(i, carry):
        columns = lanes(i * GATHER, GATHER)
        high, low = split(current[...])
        chosen = one_hot(i * GATHER, GATHER)
        spec_v[:, columns] = jnp.dot(high, chosen, preferred_element_type=f32) + jnp.dot(
            low, chosen, preferred_element_type=f32
        )
        return carry

    lax.fori_loop(0, spectrum.shape[1] // GATHER, place, 0)

    def finish(c, carry):
        every = o_all.at[:, pl.ds(0, (n_spec - 1) * CHUNK)]
        pltpu.make_async_copy(every, every, back_recv.at[c]).wait()
        kept = o_all.at[:, pl.ds(0, CHUNK)]
        pltpu.make_async_copy(kept, kept, keep_sem.at[c]).wait()
        for s in range(n_spec):
            columns = lanes(s * nodes + c * CHUNK, CHUNK)
            o_all[:, columns] += spec_v[:, columns]
        return carry

    lax.fori_loop(0, n_chunks, finish, 0)

    sent = spectrum.at[:, pl.ds(0, (n_spec - 1) * nodes)]
    pltpu.make_async_copy(sent, sent, go_send).wait()
    sent = y_all.at[pl.ds(0, (n_spec - 1) * rows), :]
    pltpu.make_async_copy(sent, sent, back_send).wait()
    pltpu.make_async_copy(others, others, dom_send).wait()


def solution(mesh):
    n_dom, n_spec = mesh.shape["dom"], mesh.shape["spec"]

    def shards(
        spectrum,
        cond,
        cap,
        block_cond,
        block_cap,
        bound,
        sources,
        used,
        couple_cond,
        couple_cap,
    ):
        rows = spectrum.shape[0]
        length, nodes = cond.shape
        n_bound = bound.shape[1]
        n_chunks = nodes // CHUNK
        tables = [jnp.asarray(t) for t in fourier_tables(length)]
        couple_cond, couple_cap = couple_cond[0], couple_cap[0]
        anywhere = pl.BlockSpec(memory_space=pl.ANY)
        vmem = pl.BlockSpec(memory_space=pltpu.VMEM)
        smem = pl.BlockSpec(memory_space=pltpu.SMEM)
        dma = pltpu.SemaphoreType.DMA
        return pl.pallas_call(
            functools.partial(kernel, n_dom, n_spec),
            out_shape=pltpu.VMEM(spectrum.shape, f32),
            in_specs=[anywhere] * 5 + [vmem, smem, smem] + [anywhere] * 4,
            out_specs=vmem,
            scratch_shapes=[
                pltpu.VMEM((length, nodes), f32),
                pltpu.VMEM((length, nodes), f32),
                pltpu.VMEM(spectrum.shape, f32),
                pltpu.VMEM(cond.shape, f32),
                pltpu.VMEM(cap.shape, f32),
                pltpu.VMEM(block_cond.shape, f32),
                pltpu.VMEM(block_cap.shape, f32),
                pltpu.VMEM(couple_cond.shape, f32),
                pltpu.VMEM(couple_cap.shape, f32),
            ]
            + [pltpu.VMEM(t.shape, f32) for t in tables]
            + [pltpu.VMEM(t.shape, bf16) for t in tables for _ in range(2)]
            + [
                pltpu.VMEM((n_dom, rows, n_bound), f32),
                pltpu.VMEM((n_bound, 1), f32),
                pltpu.VMEM((rows, n_bound), f32),
                dma((9,)),
                dma,
                dma((n_chunks,)),
                dma,
                dma((n_chunks,)),
                dma,
                dma((n_chunks,)),
                dma,
                dma,
            ],
            compiler_params=pltpu.CompilerParams(
                collective_id=0, has_side_effects=True, vmem_limit_bytes=56 * 1024 * 1024
            ),
            cost_estimate=pl.CostEstimate(
                flops=6 * length * nodes * (4 * length), bytes_accessed=20 << 20, transcendentals=0
            ),
        )(
            spectrum,
            cond,
            cap,
            block_cond,
            block_cap,
            bound,
            sources,
            used,
            couple_cond,
            couple_cap,
            *tables,
        )

    return jax.shard_map(
        shards,
        mesh=mesh,
        in_specs=(
            P("spec", "dom"),
            P(None, ("dom", "spec")),
            P(None, ("dom", "spec")),
            P(("dom", "spec"), None, None),
            P(("dom", "spec"), None, None),
            P("dom", None),
            P("dom", None),
            P("dom"),
            P("dom", None, None, None),
            P("dom", None, None, None),
        ),
        out_specs=P("spec", "dom"),
        check_vma=False,
    )
```

```python
import functools
import math

import jax
import jax.numpy as jnp
import numpy as np
from jax import lax
from jax.experimental import pallas as pl
from jax.experimental.pallas import tpu as pltpu
from jax.sharding import PartitionSpec as P

MESH = pl.DeviceIdType.MESH
CHUNK = 512
AHEAD = 4
GATHER = 2048
f32 = jnp.float32
bf16 = jnp.bfloat16


def fourier_tables(length):
    ids = np.arange(length)
    harmonic = np.where(ids == 1, length // 2, ids // 2)
    phase = (ids[:, None] * harmonic[None, :]) % length
    angles = phase * (2.0 * math.pi / length)
    is_sine = (ids % 2 == 1) & (ids >= 2)
    basis = np.where(is_sine[None, :], np.sin(angles), np.cos(angles))
    forward = basis.T * np.where(ids < 2, 1.0 / length, 2.0 / length)[:, None]
    frequency = np.where(ids >= 2, (ids // 2) * (2.0 / length), 0.0)[:, None]
    swapped = forward.reshape(length // 2, 2, length)[:, ::-1].reshape(length, length)
    slope = np.where((ids % 2 == 0)[:, None], frequency, -frequency) * swapped
    both = np.concatenate([forward, slope], axis=1)
    return basis.astype(np.float32), both.astype(np.float32)


def split(values):
    high = values.astype(bf16)
    return high, (values - high.astype(f32)).astype(bf16)


def dot3(left, right, dims=(((1,), (0,)), ((), ()))):
    dot = functools.partial(lax.dot_general, dimension_numbers=dims, preferred_element_type=f32)
    return dot(left[0], right[0]) + (dot(left[0], right[1]) + dot(left[1], right[0]))


BOTH_LANES = (((1,), (1,)), ((), ()))


def derivative(values, first_row, length):
    rows = values.shape[0]
    ids = first_row + lax.broadcasted_iota(jnp.int32, (rows, 1), 0)
    frequency = (ids // 2).astype(f32) * (2.0 / length)
    even = ids % 2 == 0
    from_next = jnp.where(even, frequency, 0.0)
    from_last = jnp.where(even, 0.0, -frequency)
    return from_next * pltpu.roll(values, rows - 1, 0) + from_last * pltpu.roll(values, 1, 0)


def kernel(
    n_dom,
    n_spec,
    spectrum,
    cond,
    cap,
    block_cond,
    block_cap,
    bound,
    sources,
    used,
    couple_cond,
    couple_cap,
    basis,
    forward,
    o_all,
    x_all,
    y_all,
    spec_v,
    cond_v,
    cap_v,
    bcond_v,
    bcap_v,
    ccond_v,
    ccap_v,
    basis_v,
    forward_v,
    basis_hv,
    basis_lv,
    fwd_hv,
    fwd_lv,
    bound_v,
    sources_v,
    used_v,
    gathered,
    bound_col,
    current,
    load_sem,
    own_sem,
    keep_sem,
    go_send,
    go_recv,
    back_send,
    back_recv,
    dom_send,
    dom_recv,
):
    rows = spectrum.shape[0]
    length, nodes = cond.shape
    n_bound = bound.shape[1]
    n_chunks = nodes // CHUNK
    dom = lax.axis_index("dom")
    me = lax.axis_index("spec")
    my_row = pl.multiple_of(me * rows, rows)

    def spec_peer(k):
        return lax.rem(me + k, n_spec)

    barrier = pltpu.get_barrier_semaphore()
    for k in range(1, n_spec):
        pl.semaphore_signal(barrier, inc=1, device_id=(dom, spec_peer(k)), device_id_type=MESH)
    for k in range(1, n_dom):
        pl.semaphore_signal(
            barrier, inc=1, device_id=(lax.rem(dom + k, n_dom), me), device_id_type=MESH
        )
    def lanes(first, size):
        return pl.ds(pl.multiple_of(first, size), size)

    loads = [
        pltpu.make_async_copy(source, target, load_sem.at[i])
        for i, (source, target) in enumerate(
            [
                (bound, bound_v),
                (spectrum, spec_v),
                (couple_cond, ccond_v),
                (couple_cap, ccap_v),
                (basis, basis_v),
                (forward, forward_v),
                (cond, cond_v),
                (cap, cap_v),
                (block_cond, bcond_v),
                (block_cap, bcap_v),
                (sources, sources_v),
                (used, used_v),
            ]
        )
    ]
    own = pltpu.make_async_copy(
        spectrum.at[:, lanes(me * nodes, nodes)], x_all.at[pl.ds(my_row, rows), :], own_sem
    )
    for copy in loads:
        copy.start()
    own.start()

    pl.semaphore_wait(barrier, n_spec - 1 + n_dom - 1)

    def send_go(c, carry):
        for k in range(1, n_spec):
            peer = spec_peer(k)
            pltpu.make_async_remote_copy(
                src_ref=spectrum.at[:, lanes(peer * nodes + c * CHUNK, CHUNK)],
                dst_ref=x_all.at[pl.ds(my_row, rows), lanes(c * CHUNK, CHUNK)],
                send_sem=go_send,
                recv_sem=go_recv.at[c],
                device_id=(dom, peer),
                device_id_type=MESH,
            ).start()
        return carry

    ahead = min(AHEAD, n_chunks)
    lax.fori_loop(0, ahead, send_go, 0)

    loads[0].wait()
    square = (n_bound, n_bound)
    diagonal = lax.broadcasted_iota(jnp.int32, square, 0) == lax.broadcasted_iota(
        jnp.int32, square, 1
    )
    spread = jnp.broadcast_to(bound_v[...], square)
    bound_col[...] = jnp.sum(jnp.where(diagonal, spread.astype(f32), 0.0), axis=1, keepdims=True)

    def one_hot(first, size):
        ids = (first + lax.broadcasted_iota(jnp.int32, (n_bound, size), 1)).astype(f32)
        return jnp.where(ids == bound_col[...], 1.0, 0.0).astype(bf16)

    loads[1].wait()

    def pick(i, total):
        columns = lanes(i * GATHER, GATHER)
        high, low = split(spec_v[:, columns])
        both = jnp.concatenate([high, low], axis=0)
        return total + lax.dot_general(
            both, one_hot(i * GATHER, GATHER), BOTH_LANES, preferred_element_type=f32
        )

    picked = lax.fori_loop(
        0, spectrum.shape[1] // GATHER, pick, jnp.zeros((2 * rows, n_bound), f32)
    )
    gathered[dom] = picked[:rows] + picked[rows:]
    for k in range(1, n_dom):
        pltpu.make_async_remote_copy(
            src_ref=gathered.at[dom],
            dst_ref=gathered.at[dom],
            send_sem=dom_send,
            recv_sem=dom_recv,
            device_id=(lax.rem(dom + k, n_dom), me),
            device_id_type=MESH,
        ).start()

    for copy in loads[2:]:
        copy.wait()
    own.wait()
    basis_hv[...], basis_lv[...] = split(basis_v[...])
    fwd_hv[...], fwd_lv[...] = split(forward_v[...])

    def work(c, carry):
        columns = lanes(c * CHUNK, CHUNK)
        arrived = x_all.at[pl.ds(0, (n_spec - 1) * rows), columns]
        pltpu.make_async_copy(arrived, arrived, go_recv.at[c]).wait()

        @pl.when(c + ahead < n_chunks)
        def _():
            send_go(c + ahead, 0)

        x = x_all[:, columns]
        wave = dot3((basis_hv[...], basis_lv[...]), split(x))
        both = jnp.concatenate([cond_v[:, columns] * wave, cap_v[:, columns] * wave], axis=0)
        y = dot3((fwd_hv[...], fwd_lv[...]), split(both))
        slope = derivative(x, 0, length)
        size = bcond_v.shape[1]
        parts = []
        for b in range(CHUNK // size):
            block = c * (CHUNK // size) + b
            here = slice(b * size, (b + 1) * size)
            pair = jnp.concatenate([x[:, here], slope[:, here]], axis=1)
            matrix = jnp.concatenate([bcond_v[block], bcap_v[block]], axis=1)
            parts.append(y[:, here] + dot3(split(pair), split(matrix), BOTH_LANES))
        y_all[:, columns] = jnp.concatenate(parts, axis=1)
        target = lanes(me * nodes + c * CHUNK, CHUNK)
        for k in range(1, n_spec):
            peer = spec_peer(k)
            pltpu.make_async_remote_copy(
                src_ref=y_all.at[pl.ds(pl.multiple_of(peer * rows, rows), rows), columns],
                dst_ref=o_all.at[:, target],
                send_sem=back_send,
                recv_sem=back_recv.at[c],
                device_id=(dom, peer),
                device_id_type=MESH,
            ).start()
        pltpu.make_async_copy(
            y_all.at[pl.ds(my_row, rows), columns], o_all.at[:, target], keep_sem.at[c]
        ).start()
        return carry

    lax.fori_loop(0, n_chunks, work, 0)

    others = gathered.at[pl.ds(0, n_dom - 1)]
    pltpu.make_async_copy(others, others, dom_recv).wait()
    total = jnp.zeros((rows, n_bound), f32)
    for c in range(sources.shape[1]):
        value = jnp.zeros((rows, n_bound), f32)
        for p in range(n_dom):
            chosen = jnp.where((sources_v[:, c : c + 1] == p) & (used_v[0] > c), 1.0, 0.0)
            value = value + chosen * gathered[p]
        slope = derivative(value, me * rows, length)
        total = total + dot3(split(value), split(ccond_v[c]), BOTH_LANES)
        total = total + dot3(split(slope), split(ccap_v[c]), BOTH_LANES)
    current[...] = total

    def place(i, carry):
        columns = lanes(i * GATHER, GATHER)
        high, low = split(current[...])
        chosen = one_hot(i * GATHER, GATHER)
        spec_v[:, columns] = jnp.dot(high, chosen, preferred_element_type=f32) + jnp.dot(
            low, chosen, preferred_element_type=f32
        )
        return carry

    lax.fori_loop(0, spectrum.shape[1] // GATHER, place, 0)

    def finish(c, carry):
        every = o_all.at[:, pl.ds(0, (n_spec - 1) * CHUNK)]
        pltpu.make_async_copy(every, every, back_recv.at[c]).wait()
        kept = o_all.at[:, pl.ds(0, CHUNK)]
        pltpu.make_async_copy(kept, kept, keep_sem.at[c]).wait()
        for s in range(n_spec):
            columns = lanes(s * nodes + c * CHUNK, CHUNK)
            o_all[:, columns] += spec_v[:, columns]
        return carry

    lax.fori_loop(0, n_chunks, finish, 0)

    sent = spectrum.at[:, pl.ds(0, (n_spec - 1) * nodes)]
    pltpu.make_async_copy(sent, sent, go_send).wait()
    sent = y_all.at[pl.ds(0, (n_spec - 1) * rows), :]
    pltpu.make_async_copy(sent, sent, back_send).wait()
    pltpu.make_async_copy(others, others, dom_send).wait()


def solution(mesh):
    n_dom, n_spec = mesh.shape["dom"], mesh.shape["spec"]

    def shards(
        spectrum,
        cond,
        cap,
        block_cond,
        block_cap,
        bound,
        sources,
        used,
        couple_cond,
        couple_cap,
    ):
        rows = spectrum.shape[0]
        length, nodes = cond.shape
        n_bound = bound.shape[1]
        n_chunks = nodes // CHUNK
        tables = [jnp.asarray(t) for t in fourier_tables(length)]
        couple_cond, couple_cap = couple_cond[0], couple_cap[0]
        anywhere = pl.BlockSpec(memory_space=pl.ANY)
        vmem = pl.BlockSpec(memory_space=pltpu.VMEM)
        dma = pltpu.SemaphoreType.DMA
        return pl.pallas_call(
            functools.partial(kernel, n_dom, n_spec),
            out_shape=pltpu.VMEM(spectrum.shape, f32),
            in_specs=[anywhere] * 12,
            out_specs=vmem,
            scratch_shapes=[
                pltpu.VMEM((length, nodes), f32),
                pltpu.VMEM((length, nodes), f32),
                pltpu.VMEM(spectrum.shape, f32),
                pltpu.VMEM(cond.shape, f32),
                pltpu.VMEM(cap.shape, f32),
                pltpu.VMEM(block_cond.shape, f32),
                pltpu.VMEM(block_cap.shape, f32),
                pltpu.VMEM(couple_cond.shape, f32),
                pltpu.VMEM(couple_cap.shape, f32),
            ]
            + [pltpu.VMEM(t.shape, f32) for t in tables]
            + [pltpu.VMEM(t.shape, bf16) for t in tables for _ in range(2)]
            + [
                pltpu.VMEM(bound.shape, jnp.int32),
                pltpu.VMEM(sources.shape, jnp.int32),
                pltpu.SMEM((1,), jnp.int32),
                pltpu.VMEM((n_dom, rows, n_bound), f32),
                pltpu.VMEM((n_bound, 1), f32),
                pltpu.VMEM((rows, n_bound), f32),
                dma((12,)),
                dma,
                dma((n_chunks,)),
                dma,
                dma((n_chunks,)),
                dma,
                dma((n_chunks,)),
                dma,
                dma,
            ],
            compiler_params=pltpu.CompilerParams(
                collective_id=0, has_side_effects=True, vmem_limit_bytes=56 * 1024 * 1024
            ),
            cost_estimate=pl.CostEstimate(
                flops=6 * length * nodes * (4 * length), bytes_accessed=20 << 20, transcendentals=0
            ),
        )(
            spectrum,
            cond,
            cap,
            block_cond,
            block_cap,
            bound,
            sources,
            used,
            couple_cond,
            couple_cap,
            *tables,
        )

    return jax.shard_map(
        shards,
        mesh=mesh,
        in_specs=(
            P("spec", "dom"),
            P(None, ("dom", "spec")),
            P(None, ("dom", "spec")),
            P(("dom", "spec"), None, None),
            P(("dom", "spec"), None, None),
            P("dom", None),
            P("dom", None),
            P("dom"),
            P("dom", None, None, None),
            P("dom", None, None, None),
        ),
        out_specs=P("spec", "dom"),
        check_vma=False,
    )
```

```python
import functools
import math

import jax
import jax.numpy as jnp
import numpy as np
from jax import lax
from jax.experimental import pallas as pl
from jax.experimental.pallas import tpu as pltpu
from jax.sharding import PartitionSpec as P

MESH = pl.DeviceIdType.MESH
CHUNK = 512
AHEAD = 4
GATHER = 2048
f32 = jnp.float32
bf16 = jnp.bfloat16


def fourier_tables(length):
    ids = np.arange(length)
    harmonic = np.where(ids == 1, length // 2, ids // 2)
    phase = (ids[:, None] * harmonic[None, :]) % length
    angles = phase * (2.0 * math.pi / length)
    is_sine = (ids % 2 == 1) & (ids >= 2)
    basis = np.where(is_sine[None, :], np.sin(angles), np.cos(angles))
    forward = basis.T * np.where(ids < 2, 1.0 / length, 2.0 / length)[:, None]
    frequency = np.where(ids >= 2, (ids // 2) * (2.0 / length), 0.0)[:, None]
    swapped = forward.reshape(length // 2, 2, length)[:, ::-1].reshape(length, length)
    slope = np.where((ids % 2 == 0)[:, None], frequency, -frequency) * swapped
    both = np.concatenate([forward, slope], axis=1)
    return basis.astype(np.float32), both.astype(np.float32)


def split(values):
    high = values.astype(bf16)
    return high, (values - high.astype(f32)).astype(bf16)


def dot3(left, right, dims=(((1,), (0,)), ((), ()))):
    dot = functools.partial(lax.dot_general, dimension_numbers=dims, preferred_element_type=f32)
    return dot(left[0], right[0]) + (dot(left[0], right[1]) + dot(left[1], right[0]))


BOTH_LANES = (((1,), (1,)), ((), ()))


def derivative(values, first_row, length):
    rows = values.shape[0]
    ids = first_row + lax.broadcasted_iota(jnp.int32, (rows, 1), 0)
    frequency = (ids // 2).astype(f32) * (2.0 / length)
    even = ids % 2 == 0
    from_next = jnp.where(even, frequency, 0.0)
    from_last = jnp.where(even, 0.0, -frequency)
    return from_next * pltpu.roll(values, rows - 1, 0) + from_last * pltpu.roll(values, 1, 0)


def kernel(
    n_dom,
    n_spec,
    spectrum,
    cond,
    cap,
    block_cond,
    block_cap,
    bound,
    sources,
    used,
    couple_cond,
    couple_cap,
    basis,
    forward,
    o_all,
    x_all,
    y_all,
    spec_v,
    cond_v,
    cap_v,
    bcond_v,
    bcap_v,
    ccond_v,
    ccap_v,
    basis_v,
    forward_v,
    basis_hv,
    basis_lv,
    fwd_hv,
    fwd_lv,
    bound_v,
    sources_v,
    used_v,
    gathered,
    bound_col,
    current,
    load_sem,
    own_sem,
    keep_sem,
    go_send,
    go_recv,
    back_send,
    back_recv,
    dom_send,
    dom_recv,
):
    rows = spectrum.shape[0]
    length, nodes = cond.shape
    n_bound = bound.shape[1]
    n_chunks = nodes // CHUNK
    dom = lax.axis_index("dom")
    me = lax.axis_index("spec")
    my_row = pl.multiple_of(me * rows, rows)

    def spec_peer(k):
        return lax.rem(me + k, n_spec)

    barrier = pltpu.get_barrier_semaphore()
    for k in range(1, n_spec):
        pl.semaphore_signal(barrier, inc=1, device_id=(dom, spec_peer(k)), device_id_type=MESH)
    for k in range(1, n_dom):
        pl.semaphore_signal(
            barrier, inc=1, device_id=(lax.rem(dom + k, n_dom), me), device_id_type=MESH
        )
    def lanes(first, size):
        return pl.ds(pl.multiple_of(first, size), size)

    loads = [
        pltpu.make_async_copy(source, target, load_sem.at[i])
        for i, (source, target) in enumerate(
            [
                (bound, bound_v),
                (spectrum, spec_v),
                (couple_cond, ccond_v),
                (couple_cap, ccap_v),
                (basis, basis_v),
                (forward, forward_v),
                (cond, cond_v),
                (cap, cap_v),
                (block_cond, bcond_v),
                (block_cap, bcap_v),
                (sources, sources_v),
                (used, used_v),
            ]
        )
    ]
    own = pltpu.make_async_copy(
        spectrum.at[:, lanes(me * nodes, nodes)], x_all.at[pl.ds(my_row, rows), :], own_sem
    )
    loads[0].start()

    pl.semaphore_wait(barrier, n_spec - 1 + n_dom - 1)

    def send_go(c, carry):
        for k in range(1, n_spec):
            peer = spec_peer(k)
            pltpu.make_async_remote_copy(
                src_ref=spectrum.at[:, lanes(peer * nodes + c * CHUNK, CHUNK)],
                dst_ref=x_all.at[pl.ds(my_row, rows), lanes(c * CHUNK, CHUNK)],
                send_sem=go_send,
                recv_sem=go_recv.at[c],
                device_id=(dom, peer),
                device_id_type=MESH,
            ).start()
        return carry

    ahead = min(AHEAD, n_chunks)
    send_go(0, 0)
    own.start()
    for copy in loads[1:]:
        copy.start()
    lax.fori_loop(1, ahead, send_go, 0)

    loads[0].wait()
    square = (n_bound, n_bound)
    diagonal = lax.broadcasted_iota(jnp.int32, square, 0) == lax.broadcasted_iota(
        jnp.int32, square, 1
    )
    spread = jnp.broadcast_to(bound_v[...], square)
    bound_col[...] = jnp.sum(jnp.where(diagonal, spread.astype(f32), 0.0), axis=1, keepdims=True)

    def one_hot(first, size):
        ids = (first + lax.broadcasted_iota(jnp.int32, (n_bound, size), 1)).astype(f32)
        return jnp.where(ids == bound_col[...], 1.0, 0.0).astype(bf16)

    loads[1].wait()

    def pick(i, total):
        columns = lanes(i * GATHER, GATHER)
        high, low = split(spec_v[:, columns])
        both = jnp.concatenate([high, low], axis=0)
        return total + lax.dot_general(
            both, one_hot(i * GATHER, GATHER), BOTH_LANES, preferred_element_type=f32
        )

    picked = lax.fori_loop(
        0, spectrum.shape[1] // GATHER, pick, jnp.zeros((2 * rows, n_bound), f32)
    )
    gathered[dom] = picked[:rows] + picked[rows:]
    for k in range(1, n_dom):
        pltpu.make_async_remote_copy(
            src_ref=gathered.at[dom],
            dst_ref=gathered.at[dom],
            send_sem=dom_send,
            recv_sem=dom_recv,
            device_id=(lax.rem(dom + k, n_dom), me),
            device_id_type=MESH,
        ).start()

    for copy in loads[2:]:
        copy.wait()
    own.wait()
    basis_hv[...], basis_lv[...] = split(basis_v[...])
    fwd_hv[...], fwd_lv[...] = split(forward_v[...])

    def work(c, carry):
        columns = lanes(c * CHUNK, CHUNK)
        arrived = x_all.at[pl.ds(0, (n_spec - 1) * rows), columns]
        pltpu.make_async_copy(arrived, arrived, go_recv.at[c]).wait()

        @pl.when(c + ahead < n_chunks)
        def _():
            send_go(c + ahead, 0)

        x = x_all[:, columns]
        wave = dot3((basis_hv[...], basis_lv[...]), split(x))
        both = jnp.concatenate([cond_v[:, columns] * wave, cap_v[:, columns] * wave], axis=0)
        y = dot3((fwd_hv[...], fwd_lv[...]), split(both))
        slope = derivative(x, 0, length)
        size = bcond_v.shape[1]
        parts = []
        for b in range(CHUNK // size):
            block = c * (CHUNK // size) + b
            here = slice(b * size, (b + 1) * size)
            pair = jnp.concatenate([x[:, here], slope[:, here]], axis=1)
            matrix = jnp.concatenate([bcond_v[block], bcap_v[block]], axis=1)
            parts.append(y[:, here] + dot3(split(pair), split(matrix), BOTH_LANES))
        y_all[:, columns] = jnp.concatenate(parts, axis=1)
        target = lanes(me * nodes + c * CHUNK, CHUNK)
        for k in range(1, n_spec):
            peer = spec_peer(k)
            pltpu.make_async_remote_copy(
                src_ref=y_all.at[pl.ds(pl.multiple_of(peer * rows, rows), rows), columns],
                dst_ref=o_all.at[:, target],
                send_sem=back_send,
                recv_sem=back_recv.at[c],
                device_id=(dom, peer),
                device_id_type=MESH,
            ).start()
        pltpu.make_async_copy(
            y_all.at[pl.ds(my_row, rows), columns], o_all.at[:, target], keep_sem.at[c]
        ).start()
        return carry

    lax.fori_loop(0, n_chunks, work, 0)

    others = gathered.at[pl.ds(0, n_dom - 1)]
    pltpu.make_async_copy(others, others, dom_recv).wait()
    total = jnp.zeros((rows, n_bound), f32)
    for c in range(sources.shape[1]):
        value = jnp.zeros((rows, n_bound), f32)
        for p in range(n_dom):
            chosen = jnp.where((sources_v[:, c : c + 1] == p) & (used_v[0] > c), 1.0, 0.0)
            value = value + chosen * gathered[p]
        slope = derivative(value, me * rows, length)
        total = total + dot3(split(value), split(ccond_v[c]), BOTH_LANES)
        total = total + dot3(split(slope), split(ccap_v[c]), BOTH_LANES)
    current[...] = total

    def place(i, carry):
        columns = lanes(i * GATHER, GATHER)
        high, low = split(current[...])
        chosen = one_hot(i * GATHER, GATHER)
        spec_v[:, columns] = jnp.dot(high, chosen, preferred_element_type=f32) + jnp.dot(
            low, chosen, preferred_element_type=f32
        )
        return carry

    lax.fori_loop(0, spectrum.shape[1] // GATHER, place, 0)

    def finish(c, carry):
        every = o_all.at[:, pl.ds(0, (n_spec - 1) * CHUNK)]
        pltpu.make_async_copy(every, every, back_recv.at[c]).wait()
        kept = o_all.at[:, pl.ds(0, CHUNK)]
        pltpu.make_async_copy(kept, kept, keep_sem.at[c]).wait()
        for s in range(n_spec):
            columns = lanes(s * nodes + c * CHUNK, CHUNK)
            o_all[:, columns] += spec_v[:, columns]
        return carry

    lax.fori_loop(0, n_chunks, finish, 0)

    sent = spectrum.at[:, pl.ds(0, (n_spec - 1) * nodes)]
    pltpu.make_async_copy(sent, sent, go_send).wait()
    sent = y_all.at[pl.ds(0, (n_spec - 1) * rows), :]
    pltpu.make_async_copy(sent, sent, back_send).wait()
    pltpu.make_async_copy(others, others, dom_send).wait()


def solution(mesh):
    n_dom, n_spec = mesh.shape["dom"], mesh.shape["spec"]

    def shards(
        spectrum,
        cond,
        cap,
        block_cond,
        block_cap,
        bound,
        sources,
        used,
        couple_cond,
        couple_cap,
    ):
        rows = spectrum.shape[0]
        length, nodes = cond.shape
        n_bound = bound.shape[1]
        n_chunks = nodes // CHUNK
        tables = [jnp.asarray(t) for t in fourier_tables(length)]
        couple_cond, couple_cap = couple_cond[0], couple_cap[0]
        anywhere = pl.BlockSpec(memory_space=pl.ANY)
        vmem = pl.BlockSpec(memory_space=pltpu.VMEM)
        dma = pltpu.SemaphoreType.DMA
        return pl.pallas_call(
            functools.partial(kernel, n_dom, n_spec),
            out_shape=pltpu.VMEM(spectrum.shape, f32),
            in_specs=[anywhere] * 12,
            out_specs=vmem,
            scratch_shapes=[
                pltpu.VMEM((length, nodes), f32),
                pltpu.VMEM((length, nodes), f32),
                pltpu.VMEM(spectrum.shape, f32),
                pltpu.VMEM(cond.shape, f32),
                pltpu.VMEM(cap.shape, f32),
                pltpu.VMEM(block_cond.shape, f32),
                pltpu.VMEM(block_cap.shape, f32),
                pltpu.VMEM(couple_cond.shape, f32),
                pltpu.VMEM(couple_cap.shape, f32),
            ]
            + [pltpu.VMEM(t.shape, f32) for t in tables]
            + [pltpu.VMEM(t.shape, bf16) for t in tables for _ in range(2)]
            + [
                pltpu.VMEM(bound.shape, jnp.int32),
                pltpu.VMEM(sources.shape, jnp.int32),
                pltpu.SMEM((1,), jnp.int32),
                pltpu.VMEM((n_dom, rows, n_bound), f32),
                pltpu.VMEM((n_bound, 1), f32),
                pltpu.VMEM((rows, n_bound), f32),
                dma((12,)),
                dma,
                dma((n_chunks,)),
                dma,
                dma((n_chunks,)),
                dma,
                dma((n_chunks,)),
                dma,
                dma,
            ],
            compiler_params=pltpu.CompilerParams(
                collective_id=0, has_side_effects=True, vmem_limit_bytes=56 * 1024 * 1024
            ),
            cost_estimate=pl.CostEstimate(
                flops=6 * length * nodes * (4 * length), bytes_accessed=20 << 20, transcendentals=0
            ),
        )(
            spectrum,
            cond,
            cap,
            block_cond,
            block_cap,
            bound,
            sources,
            used,
            couple_cond,
            couple_cap,
            *tables,
        )

    return jax.shard_map(
        shards,
        mesh=mesh,
        in_specs=(
            P("spec", "dom"),
            P(None, ("dom", "spec")),
            P(None, ("dom", "spec")),
            P(("dom", "spec"), None, None),
            P(("dom", "spec"), None, None),
            P("dom", None),
            P("dom", None),
            P("dom"),
            P("dom", None, None, None),
            P("dom", None, None, None),
        ),
        out_specs=P("spec", "dom"),
        check_vma=False,
    )
```

```python
import functools
import math

import jax
import jax.numpy as jnp
import numpy as np
from jax import lax
from jax.experimental import pallas as pl
from jax.experimental.pallas import tpu as pltpu
from jax.sharding import PartitionSpec as P

MESH = pl.DeviceIdType.MESH
CHUNK = 256
AHEAD = 8
GATHER = 2048
f32 = jnp.float32
bf16 = jnp.bfloat16


def fourier_tables(length):
    ids = np.arange(length)
    harmonic = np.where(ids == 1, length // 2, ids // 2)
    phase = (ids[:, None] * harmonic[None, :]) % length
    angles = phase * (2.0 * math.pi / length)
    is_sine = (ids % 2 == 1) & (ids >= 2)
    basis = np.where(is_sine[None, :], np.sin(angles), np.cos(angles))
    forward = basis.T * np.where(ids < 2, 1.0 / length, 2.0 / length)[:, None]
    frequency = np.where(ids >= 2, (ids // 2) * (2.0 / length), 0.0)[:, None]
    swapped = forward.reshape(length // 2, 2, length)[:, ::-1].reshape(length, length)
    slope = np.where((ids % 2 == 0)[:, None], frequency, -frequency) * swapped
    both = np.concatenate([forward, slope], axis=1)
    return basis.astype(np.float32), both.astype(np.float32)


def split(values):
    high = values.astype(bf16)
    return high, (values - high.astype(f32)).astype(bf16)


def dot3(left, right, dims=(((1,), (0,)), ((), ()))):
    dot = functools.partial(lax.dot_general, dimension_numbers=dims, preferred_element_type=f32)
    return dot(left[0], right[0]) + (dot(left[0], right[1]) + dot(left[1], right[0]))


BOTH_LANES = (((1,), (1,)), ((), ()))


def derivative(values, first_row, length):
    rows = values.shape[0]
    ids = first_row + lax.broadcasted_iota(jnp.int32, (rows, 1), 0)
    frequency = (ids // 2).astype(f32) * (2.0 / length)
    even = ids % 2 == 0
    from_next = jnp.where(even, frequency, 0.0)
    from_last = jnp.where(even, 0.0, -frequency)
    return from_next * pltpu.roll(values, rows - 1, 0) + from_last * pltpu.roll(values, 1, 0)


def kernel(
    n_dom,
    n_spec,
    spectrum,
    cond,
    cap,
    block_cond,
    block_cap,
    bound,
    sources,
    used,
    couple_cond,
    couple_cap,
    basis,
    forward,
    o_all,
    x_all,
    y_all,
    spec_v,
    cond_v,
    cap_v,
    bcond_v,
    bcap_v,
    ccond_v,
    ccap_v,
    basis_v,
    forward_v,
    basis_hv,
    basis_lv,
    fwd_hv,
    fwd_lv,
    bound_v,
    sources_v,
    used_v,
    gathered,
    bound_col,
    current,
    load_sem,
    own_sem,
    keep_sem,
    go_send,
    go_recv,
    back_send,
    back_recv,
    dom_send,
    dom_recv,
):
    rows = spectrum.shape[0]
    length, nodes = cond.shape
    n_bound = bound.shape[1]
    n_chunks = nodes // CHUNK
    dom = lax.axis_index("dom")
    me = lax.axis_index("spec")
    my_row = pl.multiple_of(me * rows, rows)

    def spec_peer(k):
        return lax.rem(me + k, n_spec)

    barrier = pltpu.get_barrier_semaphore()
    for k in sorted(range(1, n_spec), key=lambda k: abs(k - n_spec // 2)):
        pl.semaphore_signal(barrier, inc=1, device_id=(dom, spec_peer(k)), device_id_type=MESH)
    for k in range(1, n_dom):
        pl.semaphore_signal(
            barrier, inc=1, device_id=(lax.rem(dom + k, n_dom), me), device_id_type=MESH
        )
    def lanes(first, size):
        return pl.ds(pl.multiple_of(first, size), size)

    loads = [
        pltpu.make_async_copy(source, target, load_sem.at[i])
        for i, (source, target) in enumerate(
            [
                (bound, bound_v),
                (spectrum, spec_v),
                (couple_cond, ccond_v),
                (couple_cap, ccap_v),
                (basis, basis_v),
                (forward, forward_v),
                (cond, cond_v),
                (cap, cap_v),
                (block_cond, bcond_v),
                (block_cap, bcap_v),
                (sources, sources_v),
                (used, used_v),
            ]
        )
    ]
    own = pltpu.make_async_copy(
        spectrum.at[:, lanes(me * nodes, nodes)], x_all.at[pl.ds(my_row, rows), :], own_sem
    )
    loads[0].start()

    pl.semaphore_wait(barrier, n_spec - 1 + n_dom - 1)

    def send_go(c, carry):
        for k in range(1, n_spec):
            peer = spec_peer(k)
            pltpu.make_async_remote_copy(
                src_ref=spectrum.at[:, lanes(peer * nodes + c * CHUNK, CHUNK)],
                dst_ref=x_all.at[pl.ds(my_row, rows), lanes(c * CHUNK, CHUNK)],
                send_sem=go_send,
                recv_sem=go_recv.at[c],
                device_id=(dom, peer),
                device_id_type=MESH,
            ).start()
        return carry

    ahead = min(AHEAD, n_chunks)
    send_go(0, 0)
    own.start()
    for copy in loads[1:]:
        copy.start()
    lax.fori_loop(1, ahead, send_go, 0)

    loads[0].wait()
    square = (n_bound, n_bound)
    diagonal = lax.broadcasted_iota(jnp.int32, square, 0) == lax.broadcasted_iota(
        jnp.int32, square, 1
    )
    spread = jnp.broadcast_to(bound_v[...], square)
    bound_col[...] = jnp.sum(jnp.where(diagonal, spread.astype(f32), 0.0), axis=1, keepdims=True)

    def one_hot(first, size):
        ids = (first + lax.broadcasted_iota(jnp.int32, (n_bound, size), 1)).astype(f32)
        return jnp.where(ids == bound_col[...], 1.0, 0.0).astype(bf16)

    loads[1].wait()

    def pick(i, total):
        columns = lanes(i * GATHER, GATHER)
        high, low = split(spec_v[:, columns])
        both = jnp.concatenate([high, low], axis=0)
        return total + lax.dot_general(
            both, one_hot(i * GATHER, GATHER), BOTH_LANES, preferred_element_type=f32
        )

    picked = lax.fori_loop(
        0, spectrum.shape[1] // GATHER, pick, jnp.zeros((2 * rows, n_bound), f32)
    )
    gathered[dom] = picked[:rows] + picked[rows:]
    for k in range(1, n_dom):
        pltpu.make_async_remote_copy(
            src_ref=gathered.at[dom],
            dst_ref=gathered.at[dom],
            send_sem=dom_send,
            recv_sem=dom_recv,
            device_id=(lax.rem(dom + k, n_dom), me),
            device_id_type=MESH,
        ).start()

    for copy in loads[2:]:
        copy.wait()
    own.wait()
    basis_hv[...], basis_lv[...] = split(basis_v[...])
    fwd_hv[...], fwd_lv[...] = split(forward_v[...])

    def work(c, carry):
        columns = lanes(c * CHUNK, CHUNK)
        arrived = x_all.at[pl.ds(0, (n_spec - 1) * rows), columns]
        pltpu.make_async_copy(arrived, arrived, go_recv.at[c]).wait()

        @pl.when(c + ahead < n_chunks)
        def _():
            send_go(c + ahead, 0)

        x = x_all[:, columns]
        wave = dot3((basis_hv[...], basis_lv[...]), split(x))
        both = jnp.concatenate([cond_v[:, columns] * wave, cap_v[:, columns] * wave], axis=0)
        y = dot3((fwd_hv[...], fwd_lv[...]), split(both))
        slope = derivative(x, 0, length)
        size = bcond_v.shape[1]
        parts = []
        for b in range(CHUNK // size):
            block = c * (CHUNK // size) + b
            here = slice(b * size, (b + 1) * size)
            pair = jnp.concatenate([x[:, here], slope[:, here]], axis=1)
            matrix = jnp.concatenate([bcond_v[block], bcap_v[block]], axis=1)
            parts.append(y[:, here] + dot3(split(pair), split(matrix), BOTH_LANES))
        y_all[:, columns] = jnp.concatenate(parts, axis=1)
        target = lanes(me * nodes + c * CHUNK, CHUNK)
        for k in range(1, n_spec):
            peer = spec_peer(k)
            pltpu.make_async_remote_copy(
                src_ref=y_all.at[pl.ds(pl.multiple_of(peer * rows, rows), rows), columns],
                dst_ref=o_all.at[:, target],
                send_sem=back_send,
                recv_sem=back_recv.at[c],
                device_id=(dom, peer),
                device_id_type=MESH,
            ).start()
        pltpu.make_async_copy(
            y_all.at[pl.ds(my_row, rows), columns], o_all.at[:, target], keep_sem.at[c]
        ).start()
        return carry

    lax.fori_loop(0, n_chunks, work, 0)

    others = gathered.at[pl.ds(0, n_dom - 1)]
    pltpu.make_async_copy(others, others, dom_recv).wait()
    total = jnp.zeros((rows, n_bound), f32)
    for c in range(sources.shape[1]):
        value = jnp.zeros((rows, n_bound), f32)
        for p in range(n_dom):
            chosen = jnp.where((sources_v[:, c : c + 1] == p) & (used_v[0] > c), 1.0, 0.0)
            value = value + chosen * gathered[p]
        slope = derivative(value, me * rows, length)
        total = total + dot3(split(value), split(ccond_v[c]), BOTH_LANES)
        total = total + dot3(split(slope), split(ccap_v[c]), BOTH_LANES)
    current[...] = total

    def place(i, carry):
        columns = lanes(i * GATHER, GATHER)
        high, low = split(current[...])
        chosen = one_hot(i * GATHER, GATHER)
        spec_v[:, columns] = jnp.dot(high, chosen, preferred_element_type=f32) + jnp.dot(
            low, chosen, preferred_element_type=f32
        )
        return carry

    lax.fori_loop(0, spectrum.shape[1] // GATHER, place, 0)

    def finish(c, carry):
        every = o_all.at[:, pl.ds(0, (n_spec - 1) * CHUNK)]
        pltpu.make_async_copy(every, every, back_recv.at[c]).wait()
        kept = o_all.at[:, pl.ds(0, CHUNK)]
        pltpu.make_async_copy(kept, kept, keep_sem.at[c]).wait()
        for s in range(n_spec):
            columns = lanes(s * nodes + c * CHUNK, CHUNK)
            o_all[:, columns] += spec_v[:, columns]
        return carry

    lax.fori_loop(0, n_chunks, finish, 0)

    sent = spectrum.at[:, pl.ds(0, (n_spec - 1) * nodes)]
    pltpu.make_async_copy(sent, sent, go_send).wait()
    sent = y_all.at[pl.ds(0, (n_spec - 1) * rows), :]
    pltpu.make_async_copy(sent, sent, back_send).wait()
    pltpu.make_async_copy(others, others, dom_send).wait()


def solution(mesh):
    n_dom, n_spec = mesh.shape["dom"], mesh.shape["spec"]

    def shards(
        spectrum,
        cond,
        cap,
        block_cond,
        block_cap,
        bound,
        sources,
        used,
        couple_cond,
        couple_cap,
    ):
        rows = spectrum.shape[0]
        length, nodes = cond.shape
        n_bound = bound.shape[1]
        n_chunks = nodes // CHUNK
        tables = [jnp.asarray(t) for t in fourier_tables(length)]
        couple_cond, couple_cap = couple_cond[0], couple_cap[0]
        anywhere = pl.BlockSpec(memory_space=pl.ANY)
        vmem = pl.BlockSpec(memory_space=pltpu.VMEM)
        dma = pltpu.SemaphoreType.DMA
        return pl.pallas_call(
            functools.partial(kernel, n_dom, n_spec),
            out_shape=pltpu.VMEM(spectrum.shape, f32),
            in_specs=[anywhere] * 12,
            out_specs=vmem,
            scratch_shapes=[
                pltpu.VMEM((length, nodes), f32),
                pltpu.VMEM((length, nodes), f32),
                pltpu.VMEM(spectrum.shape, f32),
                pltpu.VMEM(cond.shape, f32),
                pltpu.VMEM(cap.shape, f32),
                pltpu.VMEM(block_cond.shape, f32),
                pltpu.VMEM(block_cap.shape, f32),
                pltpu.VMEM(couple_cond.shape, f32),
                pltpu.VMEM(couple_cap.shape, f32),
            ]
            + [pltpu.VMEM(t.shape, f32) for t in tables]
            + [pltpu.VMEM(t.shape, bf16) for t in tables for _ in range(2)]
            + [
                pltpu.VMEM(bound.shape, jnp.int32),
                pltpu.VMEM(sources.shape, jnp.int32),
                pltpu.SMEM((1,), jnp.int32),
                pltpu.VMEM((n_dom, rows, n_bound), f32),
                pltpu.VMEM((n_bound, 1), f32),
                pltpu.VMEM((rows, n_bound), f32),
                dma((12,)),
                dma,
                dma((n_chunks,)),
                dma,
                dma((n_chunks,)),
                dma,
                dma((n_chunks,)),
                dma,
                dma,
            ],
            compiler_params=pltpu.CompilerParams(
                collective_id=0, has_side_effects=True, vmem_limit_bytes=56 * 1024 * 1024
            ),
            cost_estimate=pl.CostEstimate(
                flops=6 * length * nodes * (4 * length), bytes_accessed=20 << 20, transcendentals=0
            ),
        )(
            spectrum,
            cond,
            cap,
            block_cond,
            block_cap,
            bound,
            sources,
            used,
            couple_cond,
            couple_cap,
            *tables,
        )

    return jax.shard_map(
        shards,
        mesh=mesh,
        in_specs=(
            P("spec", "dom"),
            P(None, ("dom", "spec")),
            P(None, ("dom", "spec")),
            P(("dom", "spec"), None, None),
            P(("dom", "spec"), None, None),
            P("dom", None),
            P("dom", None),
            P("dom"),
            P("dom", None, None, None),
            P("dom", None, None, None),
        ),
        out_specs=P("spec", "dom"),
        check_vma=False,
    )
```

```python
import functools
import math

import jax
import jax.numpy as jnp
import numpy as np
from jax import lax
from jax.experimental import pallas as pl
from jax.experimental.pallas import tpu as pltpu
from jax.sharding import PartitionSpec as P

MESH = pl.DeviceIdType.MESH
CHUNK = 512
AHEAD = 4
GATHER = 2048
f32 = jnp.float32
bf16 = jnp.bfloat16


def fourier_tables(length):
    ids = np.arange(length)
    harmonic = np.where(ids == 1, length // 2, ids // 2)
    phase = (ids[:, None] * harmonic[None, :]) % length
    angles = phase * (2.0 * math.pi / length)
    is_sine = (ids % 2 == 1) & (ids >= 2)
    basis = np.where(is_sine[None, :], np.sin(angles), np.cos(angles))
    forward = basis.T * np.where(ids < 2, 1.0 / length, 2.0 / length)[:, None]
    frequency = np.where(ids >= 2, (ids // 2) * (2.0 / length), 0.0)[:, None]
    swapped = forward.reshape(length // 2, 2, length)[:, ::-1].reshape(length, length)
    slope = np.where((ids % 2 == 0)[:, None], frequency, -frequency) * swapped
    both = np.concatenate([forward, slope], axis=1)
    return basis.astype(np.float32), both.astype(np.float32)


def split(values):
    high = values.astype(bf16)
    return high, (values - high.astype(f32)).astype(bf16)


def dot3(left, right, dims=(((1,), (0,)), ((), ()))):
    dot = functools.partial(lax.dot_general, dimension_numbers=dims, preferred_element_type=f32)
    return dot(left[0], right[0]) + (dot(left[0], right[1]) + dot(left[1], right[0]))


BOTH_LANES = (((1,), (1,)), ((), ()))


def derivative(values, first_row, length):
    rows = values.shape[0]
    ids = first_row + lax.broadcasted_iota(jnp.int32, (rows, 1), 0)
    frequency = (ids // 2).astype(f32) * (2.0 / length)
    even = ids % 2 == 0
    from_next = jnp.where(even, frequency, 0.0)
    from_last = jnp.where(even, 0.0, -frequency)
    return from_next * pltpu.roll(values, rows - 1, 0) + from_last * pltpu.roll(values, 1, 0)


def kernel(
    n_dom,
    n_spec,
    spectrum,
    cond,
    cap,
    block_cond,
    block_cap,
    bound,
    sources,
    used,
    couple_cond,
    couple_cap,
    basis,
    forward,
    o_all,
    x_all,
    y_all,
    spec_v,
    cond_v,
    cap_v,
    bcond_v,
    bcap_v,
    ccond_v,
    ccap_v,
    basis_v,
    forward_v,
    basis_hv,
    basis_lv,
    fwd_hv,
    fwd_lv,
    bound_v,
    sources_v,
    used_v,
    gathered,
    bound_col,
    current,
    load_sem,
    own_sem,
    keep_sem,
    go_send,
    go_recv,
    back_send,
    back_recv,
    dom_send,
    dom_recv,
):
    rows = spectrum.shape[0]
    length, nodes = cond.shape
    n_bound = bound.shape[1]
    n_chunks = nodes // CHUNK
    dom = lax.axis_index("dom")
    me = lax.axis_index("spec")
    my_row = pl.multiple_of(me * rows, rows)

    def spec_peer(k):
        return lax.rem(me + k, n_spec)

    barrier = pltpu.get_barrier_semaphore()
    for k in range(1, n_spec):
        pl.semaphore_signal(barrier, inc=1, device_id=(dom, spec_peer(k)), device_id_type=MESH)
    for k in range(1, n_dom):
        pl.semaphore_signal(
            barrier, inc=1, device_id=(lax.rem(dom + k, n_dom), me), device_id_type=MESH
        )
    def lanes(first, size):
        return pl.ds(pl.multiple_of(first, size), size)

    loads = [
        pltpu.make_async_copy(source, target, load_sem.at[i])
        for i, (source, target) in enumerate(
            [
                (bound, bound_v),
                (spectrum, spec_v),
                (couple_cond, ccond_v),
                (couple_cap, ccap_v),
                (basis, basis_v),
                (forward, forward_v),
                (cond, cond_v),
                (cap, cap_v),
                (block_cond, bcond_v),
                (block_cap, bcap_v),
                (sources, sources_v),
                (used, used_v),
            ]
        )
    ]
    own = pltpu.make_async_copy(
        spectrum.at[:, lanes(me * nodes, nodes)], x_all.at[pl.ds(my_row, rows), :], own_sem
    )
    loads[0].start()

    pl.semaphore_wait(barrier, n_spec - 1 + n_dom - 1)

    def send_go(c, carry):
        for k in range(1, n_spec):
            peer = spec_peer(k)
            pltpu.make_async_remote_copy(
                src_ref=spectrum.at[:, lanes(peer * nodes + c * CHUNK, CHUNK)],
                dst_ref=x_all.at[pl.ds(my_row, rows), lanes(c * CHUNK, CHUNK)],
                send_sem=go_send,
                recv_sem=go_recv.at[c],
                device_id=(dom, peer),
                device_id_type=MESH,
            ).start()
        return carry

    ahead = min(AHEAD, n_chunks)
    send_go(0, 0)
    own.start()
    for copy in loads[1:]:
        copy.start()
    lax.fori_loop(1, ahead, send_go, 0)

    loads[0].wait()
    square = (n_bound, n_bound)
    diagonal = lax.broadcasted_iota(jnp.int32, square, 0) == lax.broadcasted_iota(
        jnp.int32, square, 1
    )
    spread = jnp.broadcast_to(bound_v[...], square)
    bound_col[...] = jnp.sum(jnp.where(diagonal, spread.astype(f32), 0.0), axis=1, keepdims=True)

    def one_hot(first, size):
        ids = (first + lax.broadcasted_iota(jnp.int32, (n_bound, size), 1)).astype(f32)
        return jnp.where(ids == bound_col[...], 1.0, 0.0).astype(bf16)

    loads[1].wait()

    def pick(i, total):
        columns = lanes(i * GATHER, GATHER)
        high, low = split(spec_v[:, columns])
        both = jnp.concatenate([high, low], axis=0)
        return total + lax.dot_general(
            both, one_hot(i * GATHER, GATHER), BOTH_LANES, preferred_element_type=f32
        )

    picked = lax.fori_loop(
        0, spectrum.shape[1] // GATHER, pick, jnp.zeros((2 * rows, n_bound), f32)
    )
    gathered[dom] = picked[:rows] + picked[rows:]
    for k in range(1, n_dom):
        pltpu.make_async_remote_copy(
            src_ref=gathered.at[dom],
            dst_ref=gathered.at[dom],
            send_sem=dom_send,
            recv_sem=dom_recv,
            device_id=(lax.rem(dom + k, n_dom), me),
            device_id_type=MESH,
        ).start()

    for copy in loads[2:]:
        copy.wait()
    own.wait()
    basis_hv[...], basis_lv[...] = split(basis_v[...])
    fwd_hv[...], fwd_lv[...] = split(forward_v[...])

    def work(c, carry):
        columns = lanes(c * CHUNK, CHUNK)
        arrived = x_all.at[pl.ds(0, (n_spec - 1) * rows), columns]
        pltpu.make_async_copy(arrived, arrived, go_recv.at[c]).wait()

        @pl.when(c + ahead < n_chunks)
        def _():
            send_go(c + ahead, 0)

        x = x_all[:, columns]
        wave = dot3((basis_hv[...], basis_lv[...]), split(x))
        both = jnp.concatenate([cond_v[:, columns] * wave, cap_v[:, columns] * wave], axis=0)
        y = dot3((fwd_hv[...], fwd_lv[...]), split(both))
        slope = derivative(x, 0, length)
        size = bcond_v.shape[1]
        parts = []
        for b in range(CHUNK // size):
            block = c * (CHUNK // size) + b
            here = slice(b * size, (b + 1) * size)
            pair = jnp.concatenate([x[:, here], slope[:, here]], axis=1)
            matrix = jnp.concatenate([bcond_v[block], bcap_v[block]], axis=1)
            parts.append(y[:, here] + dot3(split(pair), split(matrix), BOTH_LANES))
        y_all[:, columns] = jnp.concatenate(parts, axis=1)
        target = lanes(me * nodes + c * CHUNK, CHUNK)
        for k in range(1, n_spec):
            peer = spec_peer(k)
            pltpu.make_async_remote_copy(
                src_ref=y_all.at[pl.ds(pl.multiple_of(peer * rows, rows), rows), columns],
                dst_ref=o_all.at[:, target],
                send_sem=back_send,
                recv_sem=back_recv.at[c],
                device_id=(dom, peer),
                device_id_type=MESH,
            ).start()
        pltpu.make_async_copy(
            y_all.at[pl.ds(my_row, rows), columns], o_all.at[:, target], keep_sem.at[c]
        ).start()
        return carry

    lax.fori_loop(0, n_chunks, work, 0)

    others = gathered.at[pl.ds(0, n_dom - 1)]
    pltpu.make_async_copy(others, others, dom_recv).wait()
    total = jnp.zeros((rows, n_bound), f32)
    for c in range(sources.shape[1]):
        value = jnp.zeros((rows, n_bound), f32)
        for p in range(n_dom):
            chosen = jnp.where((sources_v[:, c : c + 1] == p) & (used_v[0] > c), 1.0, 0.0)
            value = value + chosen * gathered[p]
        slope = derivative(value, me * rows, length)
        total = total + dot3(split(value), split(ccond_v[c]), BOTH_LANES)
        total = total + dot3(split(slope), split(ccap_v[c]), BOTH_LANES)
    current[...] = total

    def place(i, carry):
        columns = lanes(i * GATHER, GATHER)
        high, low = split(current[...])
        chosen = one_hot(i * GATHER, GATHER)
        spec_v[:, columns] = jnp.dot(high, chosen, preferred_element_type=f32) + jnp.dot(
            low, chosen, preferred_element_type=f32
        )
        return carry

    lax.fori_loop(0, spectrum.shape[1] // GATHER, place, 0)

    def finish(c, carry):
        every = o_all.at[:, pl.ds(0, (n_spec - 1) * CHUNK)]
        pltpu.make_async_copy(every, every, back_recv.at[c]).wait()
        kept = o_all.at[:, pl.ds(0, CHUNK)]
        pltpu.make_async_copy(kept, kept, keep_sem.at[c]).wait()
        for s in range(n_spec):
            columns = lanes(s * nodes + c * CHUNK, CHUNK)
            o_all[:, columns] += spec_v[:, columns]
        return carry

    lax.fori_loop(0, n_chunks, finish, 0)

    sent = spectrum.at[:, pl.ds(0, (n_spec - 1) * nodes)]
    pltpu.make_async_copy(sent, sent, go_send).wait()
    sent = y_all.at[pl.ds(0, (n_spec - 1) * rows), :]
    pltpu.make_async_copy(sent, sent, back_send).wait()
    pltpu.make_async_copy(others, others, dom_send).wait()


def write_out(n_parts, held, out, sem):
    size = held.shape[1] // n_parts
    copies = [
        pltpu.make_async_copy(
            held.at[:, pl.ds(i * size, size)], out.at[:, pl.ds(i * size, size)], sem.at[i]
        )
        for i in range(n_parts)
    ]
    for copy in copies:
        copy.start()
    for copy in copies:
        copy.wait()


def solution(mesh):
    n_dom, n_spec = mesh.shape["dom"], mesh.shape["spec"]

    def shards(
        spectrum,
        cond,
        cap,
        block_cond,
        block_cap,
        bound,
        sources,
        used,
        couple_cond,
        couple_cap,
    ):
        rows = spectrum.shape[0]
        length, nodes = cond.shape
        n_bound = bound.shape[1]
        n_chunks = nodes // CHUNK
        tables = [jnp.asarray(t) for t in fourier_tables(length)]
        couple_cond, couple_cap = couple_cond[0], couple_cap[0]
        anywhere = pl.BlockSpec(memory_space=pl.ANY)
        vmem = pl.BlockSpec(memory_space=pltpu.VMEM)
        dma = pltpu.SemaphoreType.DMA
        held = pl.pallas_call(
            functools.partial(kernel, n_dom, n_spec),
            out_shape=pltpu.VMEM(spectrum.shape, f32),
            in_specs=[anywhere] * 12,
            out_specs=vmem,
            scratch_shapes=[
                pltpu.VMEM((length, nodes), f32),
                pltpu.VMEM((length, nodes), f32),
                pltpu.VMEM(spectrum.shape, f32),
                pltpu.VMEM(cond.shape, f32),
                pltpu.VMEM(cap.shape, f32),
                pltpu.VMEM(block_cond.shape, f32),
                pltpu.VMEM(block_cap.shape, f32),
                pltpu.VMEM(couple_cond.shape, f32),
                pltpu.VMEM(couple_cap.shape, f32),
            ]
            + [pltpu.VMEM(t.shape, f32) for t in tables]
            + [pltpu.VMEM(t.shape, bf16) for t in tables for _ in range(2)]
            + [
                pltpu.VMEM(bound.shape, jnp.int32),
                pltpu.VMEM(sources.shape, jnp.int32),
                pltpu.SMEM((1,), jnp.int32),
                pltpu.VMEM((n_dom, rows, n_bound), f32),
                pltpu.VMEM((n_bound, 1), f32),
                pltpu.VMEM((rows, n_bound), f32),
                dma((12,)),
                dma,
                dma((n_chunks,)),
                dma,
                dma((n_chunks,)),
                dma,
                dma((n_chunks,)),
                dma,
                dma,
            ],
            compiler_params=pltpu.CompilerParams(
                collective_id=0, has_side_effects=True, vmem_limit_bytes=56 * 1024 * 1024
            ),
            cost_estimate=pl.CostEstimate(
                flops=6 * length * nodes * (4 * length), bytes_accessed=20 << 20, transcendentals=0
            ),
        )(
            spectrum,
            cond,
            cap,
            block_cond,
            block_cap,
            bound,
            sources,
            used,
            couple_cond,
            couple_cap,
            *tables,
        )
        return pl.pallas_call(
            functools.partial(write_out, n_spec),
            out_shape=jax.ShapeDtypeStruct(spectrum.shape, f32),
            in_specs=[vmem],
            out_specs=anywhere,
            scratch_shapes=[dma((n_spec,))],
        )(held)

    return jax.shard_map(
        shards,
        mesh=mesh,
        in_specs=(
            P("spec", "dom"),
            P(None, ("dom", "spec")),
            P(None, ("dom", "spec")),
            P(("dom", "spec"), None, None),
            P(("dom", "spec"), None, None),
            P("dom", None),
            P("dom", None),
            P("dom"),
            P("dom", None, None, None),
            P("dom", None, None, None),
        ),
        out_specs=P("spec", "dom"),
        check_vma=False,
    )
```
